128 devices in a mesh: row: 8 (over z, core), col: 16 (over x, y).
Axes of the slice: x: 4, y: 4, z: 4, core: 2. Of those that a mesh axis runs over, the one named last changes fastest.
Arguments:
- factor_inverse: bfloat16 [2048, 2048], P(('row', 'col')), as said below
- panel_left: float32 [32768, 256], P(('row', 'col')), may hold values from -6 to 6
- panel_right: float32 [32768, 256], P(('row', 'col')), may hold values from -12 to 12
- panel_rank: int32 [16], P('row'), may hold values from 16 to 256, as said below
- left: float32 [32768, 4096], P('row', 'col'), may hold values from -6 to 6
- right: float32 [32768, 4096], P('row', 'col'), may hold values from -6 to 6
- probes: float32 [32768, 4096], P('row', 'col'), may hold values from -6 to 6
- trail_rank: int32 [16, 16], P('row', 'col'), may hold values from 16 to 256, as said below
Outputs:
- new_left: float32 [32768, 4096], P('row', 'col')
- new_right: float32 [32768, 4096], P('row', 'col')
The draws below stay inside these ranges and needn't reach their ends.
Inputs may be any that keep to these rules, and one draw needn't show every extreme that they name: `factor_inverse`: lower triangular with a positive diagonal. `panel_rank`: every rank is a multiple of 16, and some panel tile has rank 256. `trail_rank`: every rank is a multiple of 16, and some trailing tile has rank 256.
All inputs are finite; a program needn't handle non-finite values.
Results may differ from the reference program's by a relative error of at most 0.0012.
Values may be sent and summed in bfloat16 or wider, within the bound.
A program may use at most 128 MiB of HBM per device.

```python
import math
import jax
import jax.numpy as jnp
from jax import lax

NB = 2048
KMAX = 256
MT = 16


def rank_table(key, entries):
    first, second = jax.random.split(key)
    values = 16 * jax.random.randint(first, (entries,), 1, KMAX // 16 + 1)
    chosen = jax.random.randint(second, (), 0, entries)
    return jnp.where(jnp.arange(entries) == chosen, KMAX, values).astype(jnp.int32)


def draw_panel_rank(key, part):
    key = jax.random.fold_in(key, 5)
    return rank_table(key, MT)


def draw_trail_rank(key, part):
    key = jax.random.fold_in(key, 7)
    return rank_table(key, MT * MT).reshape(MT, MT)


def draw_factor_inverse(key, part):
    key = jax.random.fold_in(key, 11)
    first, second = jax.random.split(key)
    raw_values = jax.random.normal(first, (NB, NB), jnp.float32) * (0.6 / jnp.sqrt(NB * 1.0))
    diag_level = jax.random.uniform(second, (NB,), jnp.float32, 0.5, 1.0)
    positions = jnp.arange(NB)
    below = positions[:, None] > positions[None, :]
    on_diag = positions[:, None] == positions[None, :]
    result = jnp.where(below, raw_values, 0.0)
    return jnp.where(on_diag, diag_level[:, None], result).astype(jnp.bfloat16)


def level_of(key, dims, shards, smallest, largest):
    factor_of, own = 1.0, jax.random.fold_in(key, 6)
    for axis_at, blocks in shards:
        heights = jnp.exp(jax.random.uniform(jax.random.fold_in(own, axis_at), (blocks,), jnp.float32, smallest / len(shards), largest / len(shards)))
        factor_of = factor_of * jnp.repeat(heights, dims[axis_at] // blocks).reshape([-1 if axis == axis_at else 1 for axis in range(len(dims))])
    return factor_of


def noise(own_key, extent, spread, reach, shards=(), held_as=jnp.bfloat16):
    values = jax.random.normal(own_key, extent, jnp.float32) * spread
    if len(shards) > 0:
        values = level_of(own_key, extent, shards, -0.22, 0.18) * values
    return jnp.clip(values, min=-reach, max=reach).astype(held_as)


def setup_inputs(seed: int = 0) -> dict:
    streams_of = jax.random.split(jax.random.key(seed), 9)
    factor_inverse = draw_factor_inverse(jax.random.fold_in(streams_of[8], 71), 0)
    panel_left = noise(streams_of[1], (MT * NB, KMAX), 1.0, 6.0, ((0, 128),), jnp.float32)
    panel_right = noise(streams_of[2], (MT * NB, KMAX), 2.0, 12.0, ((0, 128),), jnp.float32)
    panel_rank = draw_panel_rank(jax.random.fold_in(streams_of[8], 71), 0)
    left = noise(streams_of[4], (MT * NB, MT * KMAX), 1.0, 6.0, ((0, 8), (1, 16)), jnp.float32)
    right = noise(streams_of[5], (MT * NB, MT * KMAX), 1.0, 6.0, ((0, 8), (1, 16)), jnp.float32)
    probes = noise(streams_of[6], (MT * NB, MT * KMAX), 1.0, 6.0, ((0, 8), (1, 16)), jnp.float32)
    trail_rank = draw_trail_rank(jax.random.fold_in(streams_of[8], 71), 0)
    return dict(factor_inverse=factor_inverse, panel_left=panel_left, panel_right=panel_right, panel_rank=panel_rank, left=left, right=right, probes=probes, trail_rank=trail_rank)


highest = lax.Precision.HIGHEST

def reference(factor_inverse, panel_left, panel_right, panel_rank, left, right, probes, trail_rank):
    inverse_lower = factor_inverse.astype(jnp.float32)
    columns = jnp.arange(KMAX, dtype=jnp.int32)
    panel_kept = (columns[None, :] < panel_rank[:, None]).astype(jnp.float32)
    masked_left = panel_left.reshape(MT, NB, KMAX) * panel_kept[:, None, :]
    masked_right = panel_right.reshape(MT, NB, KMAX) * panel_kept[:, None, :]
    stacked = masked_right.transpose(1, 0, 2).reshape(NB, MT * KMAX)
    solved_all = jnp.dot(inverse_lower, stacked, precision=highest)
    panel_solved = solved_all.reshape(NB, MT, KMAX).transpose(1, 0, 2)
    root_width = math.sqrt(NB)
    identity = (columns[:, None] == columns[None, :]).astype(jnp.float32)

    def update_row(row_items):
        left_row, right_row, probe_row, rank_row, row_left, row_solved = row_items
        kept_cols = (columns[None, :] < rank_row[:, None]).astype(jnp.float32)

        def to_tiles(block):
            return block.reshape(NB, MT, KMAX).transpose(1, 0, 2) * kept_cols[:, None, :]
        tile_left = to_tiles(left_row)
        tile_right = to_tiles(right_row)
        tile_probe = to_tiles(probe_row)
        panel_core = jnp.einsum('nk,qnl->qkl', row_solved, panel_solved, precision=highest) / NB
        right_probe = jnp.einsum('qnk,qnl->qkl', tile_right, tile_probe, precision=highest)
        panel_probe = jnp.einsum('qnk,qnl->qkl', masked_left, tile_probe, precision=highest)
        core_probe = jnp.einsum('qkl,qlm->qkm', panel_core, panel_probe, precision=highest)
        sampled = (jnp.einsum('qnk,qkl->qnl', tile_left, right_probe, precision=highest) - jnp.einsum('nk,qkl->qnl', row_left, core_probe, precision=highest)) / NB
        gram_matrix = jnp.einsum('qnk,qnl->qkl', sampled, sampled, precision=highest)
        gram_matrix = gram_matrix + (1.0 - kept_cols)[:, :, None] * identity
        gram_factor = jnp.linalg.cholesky(gram_matrix)
        new_basis = lax.linalg.triangular_solve(gram_factor, sampled, left_side=False, lower=True, transpose_a=True) * root_width
        left_proj = jnp.einsum('qnk,qnl->qkl', tile_left, new_basis, precision=highest)
        panel_proj = jnp.einsum('nk,qnl->qkl', row_left, new_basis, precision=highest)
        core_proj = jnp.einsum('qlk,qlm->qkm', panel_core, panel_proj, precision=highest)
        new_factor = (jnp.einsum('qnk,qkl->qnl', tile_right, left_proj, precision=highest) - jnp.einsum('qnk,qkl->qnl', masked_left, core_proj, precision=highest)) / NB
        return (new_basis.transpose(1, 0, 2).reshape(NB, MT * KMAX), new_factor.transpose(1, 0, 2).reshape(NB, MT * KMAX))
    out_left, out_right = lax.map(update_row, (left.reshape(MT, NB, MT * KMAX), right.reshape(MT, NB, MT * KMAX), probes.reshape(MT, NB, MT * KMAX), trail_rank, masked_left, panel_solved))
    return (out_left.reshape(MT * NB, MT * KMAX), out_right.reshape(MT * NB, MT * KMAX))
```

```python
import functools
import math

import jax
import jax.numpy as jnp
from jax import lax
from jax.experimental import pallas as pl
from jax.experimental.pallas import tpu as pltpu
from jax.sharding import PartitionSpec as P

MESH = pl.DeviceIdType.MESH
f32, bf16 = jnp.float32, jnp.bfloat16


def split3(a):
    hi = a.astype(bf16)
    rest = a - hi.astype(f32)
    mid = rest.astype(bf16)
    return hi, mid, (rest - mid.astype(f32)).astype(bf16)


def contract_rows(a, b):
    return lax.dot_general(a, b, (((0,), (0,)), ((), ())), preferred_element_type=f32)


def rows6(a, b):
    a0, a1, a2 = split3(a)
    b0, b1, b2 = split3(b)
    small = contract_rows(a1, b1) + contract_rows(a0, b2) + contract_rows(a2, b0)
    return (small + (contract_rows(a0, b1) + contract_rows(a1, b0))) + contract_rows(a0, b0)


def exchange(rank_ref, inv_ref, right_ref, left_ref, ug_out, uq_out, core_out,
             rb, l1, lb, wg, wq, ug, uq, acc,
             l1_s, l1_r, l_s, l_r, lf_s, lf_r, r_s, r_r, w_s, w_r, u_s, u_r,
             wo_s, wo_r, wz_s, wz_r, wc_s, wc_r, uo_s, uo_r, uz_s, uz_r, uc_s, uc_r, loc):
    row, col = lax.axis_index("row"), lax.axis_index("col")
    z, core = row // 2, row % 2
    x, y = col // 4, col % 4
    xp, xm, x2 = (x + 1) % 4, (x + 3) % 4, (x + 2) % 4
    yp, ym, y2 = (y + 1) % 4, (y + 3) % 4, (y + 2) % 4
    cx = x % 2
    chunk = cx * 4 + y
    sibling = (z * 2 + (1 - core), col)

    def at(xx, yy):
        return (row, xx * 4 + yy)

    pair = at(x + 1 - 2 * cx, y)
    up, down = ((z + 1) % 4 * 2 + core, col), ((z + 3) % 4 * 2 + core, col)

    opposite = ((z + 2) % 4 * 2 + core, col)
    home = (row, 2 * row + x // 2)
    is_home = home[1] == col
    home_half = col % 2
    at_home = col // 2 == row

    bar = pltpu.get_barrier_semaphore()

    def greet(who, skip=None):
        if skip is None:
            pl.semaphore_signal(bar, inc=1, device_id=who, device_id_type=MESH)
        else:
            @pl.when(jnp.logical_not(skip))
            def _():
                pl.semaphore_signal(bar, inc=1, device_id=who, device_id_type=MESH)

    for who in (at(xp, y), at(xm, y), at(x, yp), at(x, ym), up, down, opposite, sibling):
        greet(who)
    for j in range(8):
        src = (z * 2 + chunk % 2, core * 8 + j)
        greet(src, jnp.logical_and(src[0] == row, src[1] == col))

    @pl.when(at_home)
    def _():
        for j in range(8):
            greet((row, home_half * 8 + j), home_half * 8 + j == col)

    l_self = jnp.logical_and(chunk % 2 == core, x // 2 == core)

    rank = jnp.where(x // 2 == 0, rank_ref[0], rank_ref[1])
    keep = lax.broadcasted_iota(jnp.int32, (256, 256), 1) < rank
    rb[chunk] = jnp.where(keep, right_ref[...], 0.0)
    ug[x, y] = jnp.where(keep, left_ref[...], 0.0).reshape(2, 128, 256)
    pl.semaphore_wait(bar, 17 - jnp.where(l_self, 1, 0) - jnp.where(is_home, 1, 0))

    def remote(src, dst, ss, rs, who):
        return pltpu.make_async_remote_copy(
            src_ref=src, dst_ref=dst, send_sem=ss, recv_sem=rs, device_id=who, device_id_type=MESH)

    def send(buf, idx, ss, rs, i, who):
        remote(buf.at[idx], buf.at[idx], ss.at[i], rs.at[i], who).start()

    def arrive(buf, idx, rs, i):
        pltpu.make_async_copy(buf.at[idx], buf.at[idx], rs.at[i]).wait()

    def sent(buf, idx, ss, i):
        pltpu.make_async_copy(buf.at[idx], buf.at[idx], ss.at[i]).wait()

    own_c, pair_c = cx * 4, (1 - cx) * 4
    lo_half, hi_half = pl.ds(0, 128), pl.ds(128, 128)

    for i, who in enumerate((up, down, opposite)):
        remote(inv_ref, l1.at[z], l1_s.at[i], l1_r.at[i], who).start()

    send(rb, chunk, r_s, r_r, 0, at(x, yp))
    send(rb, chunk, r_s, r_r, 1, at(x, ym))
    send(rb, chunk, r_s, r_r, 2, pair)

    def l_second():
        arrive(l1, (z + 3) % 4, l1_r, 0)
        arrive(l1, (z + 1) % 4, l1_r, 1)
        arrive(l1, (z + 2) % 4, l1_r, 2)
        for dzz in range(4):
            zz = (z + dzz) % 4
            c = 2 * zz + core
            for dx in range(2):
                who = (z * 2 + x // 2, (c // 4 + 2 * dx) * 4 + c % 4)
                me = jnp.logical_and(who[0] == row, who[1] == col)
                src = inv_ref if dzz == 0 else l1.at[zz]

                @pl.when(jnp.logical_not(me))
                def _():
                    remote(src, lb.at[l_piece], l_s.at[dzz * 2 + dx], l_r.at[j_own], who).start()

                @pl.when(me)
                def _():
                    pltpu.make_async_copy(src, lb.at[l_piece], l_r.at[j_own]).start()

    def l_finish():
        for i in range(3):
            pltpu.make_async_copy(inv_ref, inv_ref, l1_s.at[i]).wait()
        for dzz in range(4):
            c = 2 * ((z + dzz) % 4) + core
            for dx in range(2):
                me = jnp.logical_and(z * 2 + x // 2 == row, (c // 4 + 2 * dx) * 4 + c % 4 == col)

                @pl.when(jnp.logical_not(me))
                def _():
                    pltpu.make_async_copy(inv_ref, inv_ref, l_s.at[dzz * 2 + dx]).wait()

    l_piece = pl.ds(pl.multiple_of(col * 16, 16), 16)
    j_own = col % 8

    def gather(buf, ss, rs):
        done = []

        def snd(idx, i, who):
            send(buf, idx, ss, rs, i, who)
            done.append((idx, i))

        def arr(idx, i):
            arrive(buf, idx, rs, i)

        q0, q1 = pl.ds(0, 64), pl.ds(64, 64)
        XP, XM, YP, YM = at(xp, y), at(xm, y), at(x, yp), at(x, ym)

        def s0():
            snd((x, y), 0, YP)
            snd((x, y), 1, YM)
            snd((x, y), 2, XP)
            snd((x, y), 3, XM)

        def s1():
            arr((x, ym), 0)
            snd((x, ym, 0, q0), 4, YP)
            snd((x, ym, 0), 5, XP)
            snd((x, ym, 0), 6, XM)
            snd((x, ym, 1, q0), 28, YP)

        def s2():
            arr((xm, y), 2)
            snd((xm, y, 1, q0), 20, XP)
            snd((xm, y, 1), 21, YP)
            snd((xm, y, 1), 22, YM)
            snd((xm, y, 0, q0), 12, XP)

        def s3():
            arr((x, yp), 1)
            snd((x, yp, 0, q1), 7, YM)
            snd((x, yp, 0), 8, XP)
            snd((x, yp, 0), 9, XM)
            snd((x, yp, 1, q1), 29, YM)

        def s4():
            arr((xp, y), 3)
            snd((xp, y, 1, q1), 23, XM)
            snd((xp, y, 1), 24, YP)
            snd((xp, y, 1), 25, YM)
            snd((xp, y, 0, q1), 13, XM)

        def s5():
            arr((x, y2, 0, q0), 4)
            arr((x, y2, 0, q1), 7)
            snd((x, y2, 0), 10, XP)
            snd((x, y2, 0), 11, XM)

        def s6():
            arr((x2, y, 1, q0), 20)
            arr((x2, y, 1, q1), 23)
            snd((x2, y, 1), 26, YP)
            snd((x2, y, 1), 27, YM)

        def s7():
            arr((xm, ym, 0), 5)
            snd((xm, ym, 0, q0), 14, XP)
            arr((xp, ym, 0), 6)
            snd((xp, ym, 0, q1), 15, XM)
            arr((xm, ym, 1), 21)
            snd((xm, ym, 1, q0), 30, YP)
            arr((xm, yp, 1), 22)
            snd((xm, yp, 1, q1), 31, YM)

        def s8():
            arr((xm, yp, 0), 8)
            snd((xm, yp, 0, q0), 16, XP)
            arr((xp, yp, 0), 9)
            snd((xp, yp, 0, q1), 17, XM)
            arr((xp, ym, 1), 24)
            snd((xp, ym, 1, q0), 32, YP)
            arr((xp, yp, 1), 25)
            snd((xp, yp, 1, q1), 33, YM)

        def s9():
            arr((xm, y2, 0), 10)
            snd((xm, y2, 0, q0), 18, XP)
            arr((xp, y2, 0), 11)
            snd((xp, y2, 0, q1), 19, XM)
            arr((x2, ym, 1), 26)
            snd((x2, ym, 1, q0), 34, YP)
            arr((x2, yp, 1), 27)
            snd((x2, yp, 1, q1), 35, YM)

        def s10():
            arr((x2, y, 0, q0), 12)
            arr((x2, y, 0, q1), 13)
            arr((x, y2, 1, q0), 28)
            arr((x, y2, 1, q1), 29)
            arr((x2, ym, 0, q0), 14)
            arr((x2, ym, 0, q1), 15)
            arr((xm, y2, 1, q0), 30)
            arr((xm, y2, 1, q1), 31)

        def s11():
            arr((x2, yp, 0, q0), 16)
            arr((x2, yp, 0, q1), 17)
            arr((xp, y2, 1, q0), 32)
            arr((xp, y2, 1, q1), 33)
            arr((x2, y2, 0, q0), 18)
            arr((x2, y2, 0, q1), 19)
            arr((x2, y2, 1, q0), 34)
            arr((x2, y2, 1, q1), 35)

        def finish():
            for idx, i in done:
                sent(buf, idx, ss, i)

        return [s0, s1, s2, s3, s4, s5, s6, s7, s8, s9, s10, s11], finish

    dz = (z - x + 4) % 4
    home_core = y // 2
    on_home_core = core == home_core
    halves = [pl.ds(0, 128), pl.ds(128, 128)]

    def to_home(buf, qbuf, os, orr):
        for hh in range(2):
            @pl.when(jnp.logical_not(is_home))
            def _():
                remote(buf.at[x, y, hh], qbuf.at[chunk, halves[hh]], os.at[hh], orr.at[2 * chunk + hh], home).start()

            @pl.when(is_home)
            def _():
                pltpu.make_async_copy(buf.at[x, y, hh], qbuf.at[chunk, halves[hh]], orr.at[2 * chunk + hh]).start()

    def to_home_finish(buf, os):
        for hh in range(2):
            @pl.when(jnp.logical_not(is_home))
            def _():
                pltpu.make_async_copy(buf.at[x, y, hh], buf.at[x, y, hh], os.at[hh]).wait()

    def ring(qbuf, orr, zs, zr, cs, cr):
        idx_of = lambda k: (k // 2, halves[k % 2])
        carries = lambda k: core == (home_core + k) % 2
        far_from = lambda k: 1 if (k // 2) % 2 == 0 else 3

        def src(k):
            idx = idx_of(k)

            @pl.when(jnp.logical_and(dz == 0, on_home_core))
            def _():
                arrive(qbuf, idx, orr, k)
                if k % 2 == 0:
                    send(qbuf, idx, zs, zr, k, up)
                    remote(qbuf.at[idx], qbuf.at[idx], zs.at[16 + k], zr.at[k], down).start()
                send(qbuf, idx, cs, cr, k, sibling)

            if k % 2 == 1:
                @pl.when(jnp.logical_and(dz == 0, jnp.logical_not(on_home_core)))
                def _():
                    arrive(qbuf, idx, cr, k)
                    send(qbuf, idx, zs, zr, k, up)
                    remote(qbuf.at[idx], qbuf.at[idx], zs.at[16 + k], zr.at[k], down).start()

        def near(k):
            idx = idx_of(k)

            @pl.when(jnp.logical_and(dz % 2 == 1, carries(k)))
            def _():
                arrive(qbuf, idx, zr, k)

                @pl.when(dz == far_from(k))
                def _():
                    send(qbuf, idx, zs, zr, k, up if far_from(k) == 1 else down)

                send(qbuf, idx, cs, cr, k, sibling)

        def far(k):
            idx = idx_of(k)

            @pl.when(jnp.logical_and(dz == 2, carries(k)))
            def _():
                arrive(qbuf, idx, zr, k)
                send(qbuf, idx, cs, cr, k, sibling)

        def end(k):
            waits = jnp.logical_and(jnp.logical_not(carries(k)), jnp.logical_not(jnp.logical_and(dz == 0, on_home_core)))

            @pl.when(waits)
            def _():
                arrive(qbuf, idx_of(k), cr, k)

        def finish():
            for k in range(16):
                idx = idx_of(k)

                @pl.when(jnp.logical_and(carries(k), dz == 0))
                def _():
                    sent(qbuf, idx, zs, k)
                    sent(qbuf, idx, zs, 16 + k)

                @pl.when(jnp.logical_and(carries(k), dz == far_from(k)))
                def _():
                    sent(qbuf, idx, zs, k)

                @pl.when(jnp.logical_or(jnp.logical_and(dz == 0, on_home_core), jnp.logical_and(dz != 0, carries(k))))
                def _():
                    sent(qbuf, idx, cs, k)

        return src, near, far, end, finish

    u_steps, u_finish = gather(ug, u_s, u_r)
    w_steps, w_finish = gather(wg, w_s, w_r)
    uz_src, uz_near, uz_far, uz_end, uz_finish = ring(uq, uo_r, uz_s, uz_r, uc_s, uc_r)
    wz_src, wz_near, wz_far, wz_end, wz_finish = ring(wq, wo_r, wz_s, wz_r, wc_s, wc_r)

    U = lambda *ks: [u_steps[k]() for k in ks]
    W = lambda *ks: [w_steps[k]() for k in ks]
    UZ = lambda fn, ks: [fn(k) for k in ks]
    WZ = lambda fn, ks: [fn(k) for k in ks]
    l_second()
    U(0)
    to_home(ug, uq, uo_s, uo_r)
    arrive(rb, own_c + ym, r_r, 0)
    send(rb, (own_c + ym, lo_half), r_s, r_r, 5, at(x, yp))
    arrive(rb, own_c + yp, r_r, 1)
    send(rb, (own_c + yp, hi_half), r_s, r_r, 6, at(x, ym))
    arrive(rb, pair_c + y, r_r, 2)
    send(rb, pair_c + y, r_s, r_r, 3, at(x, yp))
    send(rb, pair_c + y, r_s, r_r, 4, at(x, ym))
    arrive(rb, (own_c + y2, lo_half), r_r, 5)
    arrive(rb, (own_c + y2, hi_half), r_r, 6)
    send(rb, own_c + y2, r_s, r_r, 7, pair)
    for j in range(8):
        arrive(lb, pl.ds(pl.multiple_of(core * 128 + j * 16, 16), 16), l_r, j)
    my_half = pl.ds(pl.multiple_of(core * 128, 128), 128)
    other_half = pl.ds(pl.multiple_of(128 - core * 128, 128), 128)
    send(lb, my_half, lf_s, lf_r, 0, sibling)
    U(1, 2, 3, 4)
    UZ(uz_src, range(16))
    arrive(rb, pair_c + ym, r_r, 3)
    arrive(rb, pair_c + yp, r_r, 4)
    arrive(rb, pair_c + y2, r_r, 7)
    arrive(lb, other_half, lf_r, 0)

    acc[...] = jnp.zeros_like(acc)

    @pl.loop(0, 8)
    def _(j):
        low = lb[:, pl.ds(pl.multiple_of(j * 256, 256), 256)]
        h0, h1, h2 = split3(rb[j])
        acc[...] += (jnp.dot(low, h2, preferred_element_type=f32) + jnp.dot(low, h1, preferred_element_type=f32)) + jnp.dot(low, h0, preferred_element_type=f32)

    wg[x, y] = acc[...].reshape(2, 128, 256)
    W(0)
    to_home(wg, wq, wo_s, wo_r)
    U(5, 6)
    W(1, 2, 3, 4)
    U(7, 8)
    UZ(uz_near, range(16))
    W(5, 6)
    WZ(wz_src, range(8))
    U(9)
    W(7, 8)
    WZ(wz_src, range(8, 16))
    U(10, 11)
    UZ(uz_far, range(16))
    WZ(wz_near, range(8))
    W(9, 10)
    WZ(wz_near, range(8, 16))
    W(11)
    WZ(wz_far, range(16))
    UZ(uz_end, range(16))
    WZ(wz_end, range(16))

    for t in range(2):
        acc[...] = jnp.zeros_like(acc)

        @pl.loop(0, 8)
        def _(i):
            acc[...] += rows6(wg[2 * t + i // 4, i % 4].reshape(256, 256), wq[i])

        core_out[t] = acc[...] * (1.0 / 2048)

    outs = [pltpu.make_async_copy(ug, ug_out, loc.at[0]), pltpu.make_async_copy(uq, uq_out, loc.at[1])]
    for c in outs:
        c.start()
    sent(rb, chunk, r_s, 0)
    sent(rb, chunk, r_s, 1)
    sent(rb, chunk, r_s, 2)
    sent(rb, pair_c + y, r_s, 3)
    sent(rb, pair_c + y, r_s, 4)
    sent(rb, (own_c + ym, lo_half), r_s, 5)
    sent(rb, (own_c + yp, hi_half), r_s, 6)
    sent(rb, own_c + y2, r_s, 7)
    sent(lb, my_half, lf_s, 0)
    l_finish()

    u_finish()
    w_finish()
    uz_finish()
    to_home_finish(ug, uo_s)
    wz_finish()
    to_home_finish(wg, wo_s)
    for c in outs:
        c.wait()


def run_exchange(panel_rank, factor_inverse, panel_right, panel_left):
    dma = pltpu.SemaphoreType.DMA
    vm = pl.BlockSpec(memory_space=pltpu.VMEM)
    anyspec = pl.BlockSpec(memory_space=pl.ANY)
    return pl.pallas_call(
        exchange,
        out_shape=(
            jax.ShapeDtypeStruct((4, 4, 2, 128, 256), f32),
            jax.ShapeDtypeStruct((8, 256, 256), f32),
            jax.ShapeDtypeStruct((2, 256, 256), f32),
        ),
        in_specs=[pl.BlockSpec(memory_space=pltpu.SMEM), vm, vm, vm],
        out_specs=(anyspec, anyspec, vm),
        scratch_shapes=[
            pltpu.VMEM((8, 256, 256), f32), pltpu.VMEM((4, 16, 2048), bf16), pltpu.VMEM((256, 2048), bf16),
            pltpu.VMEM((4, 4, 2, 128, 256), f32), pltpu.VMEM((8, 256, 256), f32),
            pltpu.VMEM((4, 4, 2, 128, 256), f32), pltpu.VMEM((8, 256, 256), f32),
            pltpu.VMEM((256, 256), f32),
            dma((3,)), dma((3,)), dma((8,)), dma((8,)), dma((1,)), dma((1,)), dma((8,)), dma((8,)),
            dma((36,)), dma((36,)), dma((36,)), dma((36,)),
            dma((2,)), dma((16,)), dma((32,)), dma((16,)), dma((16,)), dma((16,)),
            dma((2,)), dma((16,)), dma((32,)), dma((16,)), dma((16,)), dma((16,)),
            dma((2,)),
        ],
        compiler_params=pltpu.CompilerParams(collective_id=0, has_side_effects=True, vmem_limit_bytes=50 << 20),
        name="exchange",
    )(panel_rank, factor_inverse, panel_right, panel_left)


def split2(a):
    hi = a.astype(bf16)
    return hi, (a - hi.astype(f32)).astype(bf16)


def mul(a, b):
    return jnp.dot(a, b, preferred_element_type=f32)


def dot3(a, b):
    a0, a1 = split2(a)
    b0, b1 = split2(b)
    return (mul(a0, b1) + mul(a1, b0)) + mul(a0, b0)


def dot6(a, b):
    a0, a1, a2 = split3(a)
    b0, b1, b2 = split3(b)
    small = mul(a1, b1) + mul(a0, b2) + mul(a2, b0)
    return (small + (mul(a0, b1) + mul(a1, b0))) + mul(a0, b0)


NB = 64


def factor_blocks(blocks):
    sub = lax.broadcasted_iota(jnp.int32, (8, 128), 0)
    lane = lax.broadcasted_iota(jnp.int32, (8, 128), 1)
    n = NB // 8
    all_rows = []
    for block in blocks:
        rows = []
        for g in range(n):
            unit = jnp.where(lane == sub + (NB + 8 * g), 1.0, 0.0)
            rows.append(jnp.concatenate([block[8 * g:8 * g + 8, :], unit[:, NB:]], axis=1))
        all_rows.append(rows)
    scales = [[None] * n for _ in blocks]
    for k in range(n):
        wide = [[[jnp.broadcast_to(rows[g][:, 8 * k + i:8 * k + i + 1], (8, 128)) for i in range(8)] if g >= k else None for g in range(n)] for rows in all_rows]
        pivots = [jnp.zeros((8, 128), f32) for _ in blocks]
        for i in range(8):
            for b, rows in enumerate(all_rows):
                w = wide[b]
                pivot = jnp.broadcast_to(w[k][i][i:i + 1, :], (8, 128))
                inverse = 1.0 / pivot
                pivots[b] = jnp.where(sub == i, pivot, pivots[b])
                row = jnp.broadcast_to(rows[k][i:i + 1, :], (8, 128))
                heads = [jnp.broadcast_to(w[k][j][i:i + 1, :], (8, 128)) for j in range(i + 1, 8)]
                for g in range(k, n):
                    factor = w[g][i] * inverse
                    if g == k:
                        factor = jnp.where(sub > i, factor, 0.0)
                    for j in range(i + 1, 8):
                        w[g][j] = w[g][j] - factor * heads[j - i - 1]
                    rows[g] = rows[g] - factor * row
        for b in range(len(blocks)):
            scales[b][k] = lax.rsqrt(pivots[b])
    return [jnp.concatenate([rows[g] * scales[b][g] for g in range(n)], axis=0)[:, NB:] for b, rows in enumerate(all_rows)]


def solve_rows(g_refs, c_refs):
    count = len(g_refs)
    for k in range(256 // NB):
        lo, hi = k * NB, (k + 1) * NB
        inverses = factor_blocks([g[lo:hi, lo:hi] for g in g_refs])
        for b in range(count):
            g, c = g_refs[b], c_refs[b]
            if hi < 256:
                gu = dot6(inverses[b], g[lo:hi, hi:])
            cu = dot6(inverses[b], c[lo:hi, :])
            c[lo:hi, :] = cu
            if hi < 256:
                gt = gu.T
                g[hi:, hi:] -= dot6(gt, gu)
                c[hi:, :] -= dot6(gt, cu)


CHUNK = 512


def tiles_kernel(rank_ref, left, right, probes, ug, uq, core, out_left, out_right,
                 xu, xv, xo, xg, xq, yl, yr, hh, hl, cc, gg, ct, ds0, ds1, es0, es1, in_sem, out_sem):
    order = 2048
    loads = []
    for t in range(2):
        rows = pl.ds(t * order, order)
        loads.append([pltpu.make_async_copy(src.at[rows], dst.at[rows], in_sem.at[4 * t + i])
                      for i, (src, dst) in enumerate(((right, xv), (probes, xo), (left, xu), (ug, xg)))])
    load_q = pltpu.make_async_copy(uq, xq, in_sem.at[8])
    load_q.start()
    for group in loads:
        for load in group:
            load.start()
    columns = lax.broadcasted_iota(jnp.int32, (256, 256), 1)
    rows_at = lax.broadcasted_iota(jnp.int32, (256, 256), 0)
    load_q.wait()
    for t in range(2):
        rank = rank_ref[t, 0]
        cc[t] = jnp.zeros((512, 256), f32)
        hh[t] = jnp.zeros((512, 512), f32)
        hl[...] = jnp.zeros((512, 512), f32)
        loads[t][0].wait()
        loads[t][1].wait()

        @pl.loop(0, order // CHUNK)
        def _(j):
            at = pl.ds(pl.multiple_of(t * order + j * CHUNK, CHUNK), CHUNK)
            atq = pl.ds(pl.multiple_of(j * CHUNK, CHUNK), CHUNK)
            o = xo[at, :]
            cc[t, :256] += dot6(xv[at, :].T, o)
            cc[t, 256:] += dot6(xq[atq, :].T, o)

        loads[t][2].wait()
        loads[t][3].wait()

        @pl.loop(0, order // CHUNK)
        def _(j):
            at = pl.ds(pl.multiple_of(t * order + j * CHUNK, CHUNK), CHUNK)
            x0, x1 = split2(jnp.concatenate([xu[at, :], xg[at, :]], axis=1))
            x0t = x0.T
            hh[t] += mul(x0t, x0)
            hl[...] += mul(x0t, x1)

        hh[t] += hl[...] + hl[...].T
        keep = columns < rank
        scale = 1.0 / order
        c1 = jnp.where(jnp.logical_and(keep, rows_at < rank), cc[t, :256], 0.0) * scale
        pp = jnp.where(keep, cc[t, 256:], 0.0) * -scale
        c2 = dot6(core[t], pp)
        c = jnp.concatenate([c1, c2], axis=0)
        cc[t] = c
        ct[t] = c.T
        hc = dot6(hh[t], c)
        unit = jnp.where(jnp.logical_and(columns == rows_at, jnp.logical_not(keep)), 1.0, 0.0)
        gg[t] = dot6(ct[t], hc) + unit
    solve_rows([gg.at[0], gg.at[1]], [ct.at[0], ct.at[1]])
    stores = []
    for t in range(2):
        rank = rank_ref[t, 0]
        d = (ct[t] * math.sqrt(order)).T
        d0, d1 = split2(d)
        ds0[t], ds1[t] = d0, d1
        h0, h1 = split2(hh[t])
        hd = (mul(h0, d1) + mul(h1, d0)) + mul(h0, d0)
        e1 = jnp.where(rows_at < rank, hd[:256], 0.0) * (1.0 / order)
        e2 = dot3(core[t].T, hd[256:]) * (-1.0 / order)
        es0[t], es1[t] = split2(jnp.concatenate([e1, e2], axis=0))

        @pl.loop(0, order // CHUNK)
        def _(j):
            at = pl.ds(pl.multiple_of(t * order + j * CHUNK, CHUNK), CHUNK)
            x0, x1 = split2(jnp.concatenate([xu[at, :], xg[at, :]], axis=1))
            yl[at, :] = (mul(x0, ds1[t]) + mul(x1, ds0[t])) + mul(x0, ds0[t])

        rows = pl.ds(t * order, order)
        stores.append(pltpu.make_async_copy(yl.at[rows], out_left.at[rows], out_sem.at[2 * t]))
        stores[-1].start()

        @pl.loop(0, order // CHUNK)
        def _(j):
            at = pl.ds(pl.multiple_of(t * order + j * CHUNK, CHUNK), CHUNK)
            atq = pl.ds(pl.multiple_of(j * CHUNK, CHUNK), CHUNK)
            x0, x1 = split2(jnp.concatenate([xv[at, :], xq[atq, :]], axis=1))
            yr[at, :] = (mul(x0, es1[t]) + mul(x1, es0[t])) + mul(x0, es0[t])

        stores.append(pltpu.make_async_copy(yr.at[rows], out_right.at[rows], out_sem.at[2 * t + 1]))
        stores[-1].start()
    for store in stores:
        store.wait()


def run_tiles(trail_rank, left, right, probes, ug, uq, core):
    hbm = pl.BlockSpec(memory_space=pl.ANY)
    vm = pl.BlockSpec(memory_space=pltpu.VMEM)
    big = pltpu.VMEM((4096, 256), f32)
    return pl.pallas_call(
        tiles_kernel,
        out_shape=(jax.ShapeDtypeStruct((4096, 256), f32),) * 2,
        in_specs=[pl.BlockSpec(memory_space=pltpu.SMEM), hbm, hbm, hbm, hbm, hbm, vm],
        out_specs=(hbm, hbm),
        scratch_shapes=[big, big, big, big, pltpu.VMEM((2048, 256), f32), big, big,
                        pltpu.VMEM((2, 512, 512), f32), pltpu.VMEM((512, 512), f32),
                        pltpu.VMEM((2, 512, 256), f32), pltpu.VMEM((2, 256, 256), f32), pltpu.VMEM((2, 256, 512), f32)]
        + [pltpu.VMEM((2, 512, 256), bf16)] * 4
        + [pltpu.SemaphoreType.DMA((9,)), pltpu.SemaphoreType.DMA((4,))],
        compiler_params=pltpu.CompilerParams(vmem_limit_bytes=56 << 20), name="tiles",
    )(trail_rank, left, right, probes, ug, uq, core)


def shards(factor_inverse, panel_left, panel_right, panel_rank, left, right, probes, trail_rank):
    ug, uq, core = run_exchange(panel_rank, factor_inverse, panel_right, panel_left)
    return run_tiles(trail_rank, left, right, probes, ug.reshape(4096, 256), uq.reshape(2048, 256), core)


def solution(mesh):
    return jax.shard_map(
        shards,
        mesh=mesh,
        in_specs=(
            P(("row", "col"), None),
            P(("row", "col"), None),
            P(("row", "col"), None),
            P("row"),
            P("row", "col"),
            P("row", "col"),
            P("row", "col"),
            P("row", "col"),
        ),
        out_specs=(P("row", "col"), P("row", "col")),
        check_vma=False,
    )
```

```python
import functools
import math

import jax
import jax.numpy as jnp
from jax import lax
from jax.experimental import pallas as pl
from jax.experimental.pallas import tpu as pltpu
from jax.sharding import PartitionSpec as P

MESH = pl.DeviceIdType.MESH
f32, bf16 = jnp.float32, jnp.bfloat16


def split3(a):
    hi = a.astype(bf16)
    rest = a - hi.astype(f32)
    mid = rest.astype(bf16)
    return hi, mid, (rest - mid.astype(f32)).astype(bf16)


def exchange(rank_ref, inv_ref, right_ref, left_ref, tiles_u, tiles_v, tiles_o, ug_out, uq_out, core_out, hh_out, cc_out,
             rb, l1, lb, wg, wq, ug, uq, acc, rtmp, xu, xv, xo, hh, hl, cc,
             l1_s, l1_r, l_s, l_r, lf_s, lf_r, r_s, r_r, w_s, w_r, u_s, u_r,
             wo_s, wo_r, wz_s, wz_r, wc_s, wc_r, uo_s, uo_r, uz_s, uz_r, uc_s, uc_r, loc, load):
    row, col = lax.axis_index("row"), lax.axis_index("col")
    z, core = row // 2, row % 2
    x, y = col // 4, col % 4
    xp, xm, x2 = (x + 1) % 4, (x + 3) % 4, (x + 2) % 4
    yp, ym, y2 = (y + 1) % 4, (y + 3) % 4, (y + 2) % 4
    cx = x % 2
    chunk = cx * 4 + y
    sibling = (z * 2 + (1 - core), col)

    def at(xx, yy):
        return (row, xx * 4 + yy)

    pair = at(x + 1 - 2 * cx, y)
    up, down = ((z + 1) % 4 * 2 + core, col), ((z + 3) % 4 * 2 + core, col)

    opposite = ((z + 2) % 4 * 2 + core, col)
    home = (row, 2 * row + x // 2)
    is_home = home[1] == col
    home_half = col % 2
    at_home = col // 2 == row

    own_loads = [pltpu.make_async_copy(src, dst, load.at[i]) for i, (src, dst) in enumerate((
        (right_ref, rtmp.at[0]), (left_ref, rtmp.at[1]), (inv_ref, l1.at[z])))]
    tile_loads = [pltpu.make_async_copy(src, dst, load.at[3 + i]) for i, (src, dst) in enumerate((
        (tiles_v, xv), (tiles_o, xo), (tiles_u, xu)))]
    for c in own_loads + tile_loads:
        c.start()

    bar = pltpu.get_barrier_semaphore()

    def greet(who, skip=None):
        if skip is None:
            pl.semaphore_signal(bar, inc=1, device_id=who, device_id_type=MESH)
        else:
            @pl.when(jnp.logical_not(skip))
            def _():
                pl.semaphore_signal(bar, inc=1, device_id=who, device_id_type=MESH)

    for who in (at(xp, y), at(xm, y), at(x, yp), at(x, ym), up, down, opposite, sibling):
        greet(who)
    for j in range(8):
        src = (z * 2 + chunk % 2, core * 8 + j)
        greet(src, jnp.logical_and(src[0] == row, src[1] == col))

    @pl.when(at_home)
    def _():
        for j in range(8):
            greet((row, home_half * 8 + j), home_half * 8 + j == col)

    l_self = jnp.logical_and(chunk % 2 == core, x // 2 == core)

    for c in own_loads:
        c.wait()
    rank = jnp.where(x // 2 == 0, rank_ref[0], rank_ref[1])
    keep = lax.broadcasted_iota(jnp.int32, (256, 256), 1) < rank
    rb[chunk] = jnp.where(keep, rtmp[0], 0.0)
    ug[x, y] = jnp.where(keep, rtmp[1], 0.0).reshape(2, 128, 256)
    pl.semaphore_wait(bar, 17 - jnp.where(l_self, 1, 0) - jnp.where(is_home, 1, 0))

    def remote(src, dst, ss, rs, who):
        return pltpu.make_async_remote_copy(
            src_ref=src, dst_ref=dst, send_sem=ss, recv_sem=rs, device_id=who, device_id_type=MESH)

    def send(buf, idx, ss, rs, i, who):
        remote(buf.at[idx], buf.at[idx], ss.at[i], rs.at[i], who).start()

    def arrive(buf, idx, rs, i):
        pltpu.make_async_copy(buf.at[idx], buf.at[idx], rs.at[i]).wait()

    def sent(buf, idx, ss, i):
        pltpu.make_async_copy(buf.at[idx], buf.at[idx], ss.at[i]).wait()

    own_c, pair_c = cx * 4, (1 - cx) * 4
    lo_half, hi_half = pl.ds(0, 128), pl.ds(128, 128)

    for i, who in enumerate((up, down, opposite)):
        remote(l1.at[z], l1.at[z], l1_s.at[i], l1_r.at[i], who).start()

    send(rb, chunk, r_s, r_r, 0, at(x, yp))
    send(rb, chunk, r_s, r_r, 1, at(x, ym))
    send(rb, chunk, r_s, r_r, 2, pair)

    def l_second():
        arrive(l1, (z + 3) % 4, l1_r, 0)
        arrive(l1, (z + 1) % 4, l1_r, 1)
        arrive(l1, (z + 2) % 4, l1_r, 2)
        for dzz in range(4):
            zz = (z + dzz) % 4
            c = 2 * zz + core
            for dx in range(2):
                who = (z * 2 + x // 2, (c // 4 + 2 * dx) * 4 + c % 4)
                me = jnp.logical_and(who[0] == row, who[1] == col)
                src = l1.at[zz]

                @pl.when(jnp.logical_not(me))
                def _():
                    remote(src, lb.at[l_piece], l_s.at[dzz * 2 + dx], l_r.at[j_own], who).start()

                @pl.when(me)
                def _():
                    pltpu.make_async_copy(src, lb.at[l_piece], l_r.at[j_own]).start()

    def l_finish():
        for i in range(3):
            pltpu.make_async_copy(l1.at[0], l1.at[0], l1_s.at[i]).wait()
        for dzz in range(4):
            c = 2 * ((z + dzz) % 4) + core
            for dx in range(2):
                me = jnp.logical_and(z * 2 + x // 2 == row, (c // 4 + 2 * dx) * 4 + c % 4 == col)

                @pl.when(jnp.logical_not(me))
                def _():
                    pltpu.make_async_copy(l1.at[0], l1.at[0], l_s.at[dzz * 2 + dx]).wait()

    l_piece = pl.ds(pl.multiple_of(col * 16, 16), 16)
    j_own = col % 8

    def gather(buf, ss, rs):
        done = []

        def snd(idx, i, who):
            send(buf, idx, ss, rs, i, who)
            done.append((idx, i))

        def arr(idx, i):
            arrive(buf, idx, rs, i)

        q0, q1 = pl.ds(0, 64), pl.ds(64, 64)
        XP, XM, YP, YM = at(xp, y), at(xm, y), at(x, yp), at(x, ym)

        def s0():
            snd((x, y), 0, YP)
            snd((x, y), 1, YM)
            snd((x, y), 2, XP)
            snd((x, y), 3, XM)

        def s1():
            arr((x, ym), 0)
            snd((x, ym, 0, q0), 4, YP)
            snd((x, ym, 0), 5, XP)
            snd((x, ym, 0), 6, XM)
            snd((x, ym, 1, q0), 28, YP)

        def s2():
            arr((xm, y), 2)
            snd((xm, y, 1, q0), 20, XP)
            snd((xm, y, 1), 21, YP)
            snd((xm, y, 1), 22, YM)
            snd((xm, y, 0, q0), 12, XP)

        def s3():
            arr((x, yp), 1)
            snd((x, yp, 0, q1), 7, YM)
            snd((x, yp, 0), 8, XP)
            snd((x, yp, 0), 9, XM)
            snd((x, yp, 1, q1), 29, YM)

        def s4():
            arr((xp, y), 3)
            snd((xp, y, 1, q1), 23, XM)
            snd((xp, y, 1), 24, YP)
            snd((xp, y, 1), 25, YM)
            snd((xp, y, 0, q1), 13, XM)

        def s5():
            arr((x, y2, 0, q0), 4)
            arr((x, y2, 0, q1), 7)
            snd((x, y2, 0), 10, XP)
            snd((x, y2, 0), 11, XM)

        def s6():
            arr((x2, y, 1, q0), 20)
            arr((x2, y, 1, q1), 23)
            snd((x2, y, 1), 26, YP)
            snd((x2, y, 1), 27, YM)

        def s7():
            arr((xm, ym, 0), 5)
            snd((xm, ym, 0, q0), 14, XP)
            arr((xp, ym, 0), 6)
            snd((xp, ym, 0, q1), 15, XM)
            arr((xm, ym, 1), 21)
            snd((xm, ym, 1, q0), 30, YP)
            arr((xm, yp, 1), 22)
            snd((xm, yp, 1, q1), 31, YM)

        def s8():
            arr((xm, yp, 0), 8)
            snd((xm, yp, 0, q0), 16, XP)
            arr((xp, yp, 0), 9)
            snd((xp, yp, 0, q1), 17, XM)
            arr((xp, ym, 1), 24)
            snd((xp, ym, 1, q0), 32, YP)
            arr((xp, yp, 1), 25)
            snd((xp, yp, 1, q1), 33, YM)

        def s9():
            arr((xm, y2, 0), 10)
            snd((xm, y2, 0, q0), 18, XP)
            arr((xp, y2, 0), 11)
            snd((xp, y2, 0, q1), 19, XM)
            arr((x2, ym, 1), 26)
            snd((x2, ym, 1, q0), 34, YP)
            arr((x2, yp, 1), 27)
            snd((x2, yp, 1, q1), 35, YM)

        def s10():
            arr((x2, y, 0, q0), 12)
            arr((x2, y, 0, q1), 13)
            arr((x, y2, 1, q0), 28)
            arr((x, y2, 1, q1), 29)
            arr((x2, ym, 0, q0), 14)
            arr((x2, ym, 0, q1), 15)
            arr((xm, y2, 1, q0), 30)
            arr((xm, y2, 1, q1), 31)

        def s11():
            arr((x2, yp, 0, q0), 16)
            arr((x2, yp, 0, q1), 17)
            arr((xp, y2, 1, q0), 32)
            arr((xp, y2, 1, q1), 33)
            arr((x2, y2, 0, q0), 18)
            arr((x2, y2, 0, q1), 19)
            arr((x2, y2, 1, q0), 34)
            arr((x2, y2, 1, q1), 35)

        def finish():
            for idx, i in done:
                sent(buf, idx, ss, i)

        return [s0, s1, s2, s3, s4, s5, s6, s7, s8, s9, s10, s11], finish

    dz = (z - x + 4) % 4
    home_core = y // 2
    on_home_core = core == home_core
    halves = [pl.ds(0, 128), pl.ds(128, 128)]

    def to_home(buf, qbuf, os, orr):
        for hh in range(2):
            @pl.when(jnp.logical_not(is_home))
            def _():
                remote(buf.at[x, y, hh], qbuf.at[chunk, halves[hh]], os.at[hh], orr.at[2 * chunk + hh], home).start()

            @pl.when(is_home)
            def _():
                pltpu.make_async_copy(buf.at[x, y, hh], qbuf.at[chunk, halves[hh]], orr.at[2 * chunk + hh]).start()

    def to_home_finish(buf, os):
        for hh in range(2):
            @pl.when(jnp.logical_not(is_home))
            def _():
                pltpu.make_async_copy(buf.at[x, y, hh], buf.at[x, y, hh], os.at[hh]).wait()

    def ring(qbuf, orr, zs, zr, cs, cr):
        idx_of = lambda k: (k // 2, halves[k % 2])
        carries = lambda k: core == (home_core + k) % 2
        onward = lambda k: up if k < 8 else down
        hop_of = lambda k: dz if k < 8 else (4 - dz) % 4
        at_source = jnp.logical_and(dz == 0, on_home_core)

        def src(k):
            idx = idx_of(k)

            @pl.when(at_source)
            def _():
                arrive(qbuf, idx, orr, k)
                if k % 2 == 0:
                    send(qbuf, idx, zs, zr, k, onward(k))
                send(qbuf, idx, cs, cr, k, sibling)

            if k % 2 == 1:
                @pl.when(jnp.logical_and(dz == 0, jnp.logical_not(on_home_core)))
                def _():
                    arrive(qbuf, idx, cr, k)
                    send(qbuf, idx, zs, zr, k, onward(k))

        def hop(number, k):
            idx = idx_of(k)

            @pl.when(jnp.logical_and(hop_of(k) == number, carries(k)))
            def _():
                arrive(qbuf, idx, zr, k)
                if number < 3:
                    send(qbuf, idx, zs, zr, k, onward(k))
                send(qbuf, idx, cs, cr, k, sibling)

        def end(k):
            waits = jnp.logical_and(jnp.logical_not(carries(k)), jnp.logical_not(at_source))

            @pl.when(waits)
            def _():
                arrive(qbuf, idx_of(k), cr, k)

        def finish():
            for k in range(16):
                idx = idx_of(k)

                @pl.when(jnp.logical_and(carries(k), hop_of(k) != 3))
                def _():
                    sent(qbuf, idx, zs, k)

                @pl.when(jnp.logical_or(at_source, jnp.logical_and(dz != 0, carries(k))))
                def _():
                    sent(qbuf, idx, cs, k)

        return src, hop, end, finish

    u_steps, u_finish = gather(ug, u_s, u_r)
    w_steps, w_finish = gather(wg, w_s, w_r)
    uz_src, uz_hop, uz_end, uz_finish = ring(uq, uo_r, uz_s, uz_r, uc_s, uc_r)
    wz_src, wz_hop, wz_end, wz_finish = ring(wq, wo_r, wz_s, wz_r, wc_s, wc_r)

    def pick(options, n):
        value = options[0]
        for i in range(1, len(options)):
            value = jnp.where(n == i, options[i], value)
        return value

    def right_probe(t):
        cc[t, :256] = jnp.zeros((256, 256), f32)

        @pl.loop(0, 4)
        def _(j):
            rows = pl.ds(pl.multiple_of(t * 2048 + j * 512, 512), 512)
            cc[t, :256] += dot6(xv[rows, :].T, xo[rows, :])

    def panel_probe(t):
        cc[t, 256:] = jnp.zeros((256, 256), f32)

        @pl.loop(0, 4)
        def _(j):
            rows = pl.ds(pl.multiple_of(t * 2048 + j * 512, 512), 512)
            cc[t, 256:] += dot6(uq[pl.ds(2 * j, 2)].reshape(512, 256).T, xo[rows, :])

    def cross(t):
        acc[...] = jnp.zeros_like(acc)

        @pl.loop(0, 4)
        def _(i):
            w = wg[2 * t + i // 2, pl.ds((i % 2) * 2, 2)].reshape(512, 256)
            acc[...] += dot6(w.T, wq[pl.ds(2 * i, 2)].reshape(512, 256))

        core_out[t] = acc[...] * (1.0 / 2048)

    def squares(places):
        @pl.loop(0, len(places))
        def _(n):
            px, py = pick([p[0] for p in places], n), pick([p[1] for p in places], n)
            rows = pl.ds(pl.multiple_of((px * 4 + py) * 256, 256), 256)
            t = px // 2
            x0, x1 = split2(jnp.concatenate([xu[rows, :], ug[px, py].reshape(256, 256)], axis=1))
            x0t = x0.T
            hh[t] += mul(x0t, x0)
            hl[t] += mul(x0t, x1)

    U = lambda *ks: [u_steps[k]() for k in ks]
    W = lambda *ks: [w_steps[k]() for k in ks]
    every = lambda fn, ks=range(16): [fn(k) for k in ks]

    to_home(ug, uq, uo_s, uo_r)
    l_second()
    tile_loads[0].wait()
    tile_loads[1].wait()
    right_probe(0)
    arrive(rb, own_c + ym, r_r, 0)
    send(rb, (own_c + ym, lo_half), r_s, r_r, 5, at(x, yp))
    arrive(rb, own_c + yp, r_r, 1)
    send(rb, (own_c + yp, hi_half), r_s, r_r, 6, at(x, ym))
    arrive(rb, pair_c + y, r_r, 2)
    send(rb, pair_c + y, r_s, r_r, 3, at(x, yp))
    send(rb, pair_c + y, r_s, r_r, 4, at(x, ym))
    arrive(rb, (own_c + y2, lo_half), r_r, 5)
    arrive(rb, (own_c + y2, hi_half), r_r, 6)
    send(rb, own_c + y2, r_s, r_r, 7, pair)
    for j in range(8):
        arrive(lb, pl.ds(pl.multiple_of(core * 128 + j * 16, 16), 16), l_r, j)
    my_half = pl.ds(pl.multiple_of(core * 128, 128), 128)
    other_half = pl.ds(pl.multiple_of(128 - core * 128, 128), 128)
    send(lb, my_half, lf_s, lf_r, 0, sibling)
    U(0)
    right_probe(1)
    tile_loads[2].wait()
    hh[...] = jnp.zeros_like(hh)
    hl[...] = jnp.zeros_like(hl)
    arrive(rb, pair_c + ym, r_r, 3)
    arrive(rb, pair_c + yp, r_r, 4)
    arrive(rb, pair_c + y2, r_r, 7)
    arrive(lb, other_half, lf_r, 0)
    acc[...] = jnp.zeros_like(acc)

    @pl.loop(0, 8)
    def _(j):
        low = lb[:, pl.ds(pl.multiple_of(j * 256, 256), 256)]
        h0, h1, h2 = split3(rb[j])
        acc[...] += (mul(low, h2) + mul(low, h1)) + mul(low, h0)

    wg[x, y] = acc[...].reshape(2, 128, 256)
    W(0)
    to_home(wg, wq, wo_s, wo_r)
    interleaved = [(n % 2) * 8 + n // 2 for n in range(16)]
    hop = lambda fn, number: [fn(number, k) for k in interleaved]
    every(uz_src, interleaved)
    W(1, 2, 3, 4)
    every(wz_src, interleaved)
    hop(uz_hop, 1)
    W(5, 6, 7, 8)
    hop(uz_hop, 2)
    hop(wz_hop, 1)
    W(9, 10)
    U(1, 2, 3, 4)
    hop(uz_hop, 3)
    hop(wz_hop, 2)
    W(11)
    every(uz_end)
    panel_probe(0)
    U(5, 6)
    hop(wz_hop, 3)
    squares([(x, y), (x, ym), (xm, y), (x, yp), (xp, y)])
    U(7, 8)
    panel_probe(1)
    every(wz_end)
    cross(0)
    U(9)
    cross(1)
    U(10)
    squares([(xm, ym), (xp, ym), (xm, yp), (xp, yp), (x2, y), (x, y2), (x2, ym), (xm, y2)])
    U(11)
    outs = [pltpu.make_async_copy(src, dst, loc.at[i]) for i, (src, dst) in enumerate((
        (ug, ug_out), (uq, uq_out), (cc, cc_out), (hh, hh_out)))]
    for c in outs[:3]:
        c.start()
    squares([(x2, yp), (xp, y2), (x2, y2)])
    for t in range(2):
        hh[t] += hl[t] + hl[t].T
    outs[3].start()
    sent(rb, chunk, r_s, 0)
    sent(rb, chunk, r_s, 1)
    sent(rb, chunk, r_s, 2)
    sent(rb, pair_c + y, r_s, 3)
    sent(rb, pair_c + y, r_s, 4)
    sent(rb, (own_c + ym, lo_half), r_s, 5)
    sent(rb, (own_c + yp, hi_half), r_s, 6)
    sent(rb, own_c + y2, r_s, 7)
    sent(lb, my_half, lf_s, 0)
    l_finish()

    u_finish()
    w_finish()
    uz_finish()
    to_home_finish(ug, uo_s)
    wz_finish()
    to_home_finish(wg, wo_s)
    for c in outs:
        c.wait()


def run_exchange(panel_rank, factor_inverse, panel_right, panel_left, left, right, probes):
    dma = pltpu.SemaphoreType.DMA
    vm = pl.BlockSpec(memory_space=pltpu.VMEM)
    hbm = pl.BlockSpec(memory_space=pl.ANY)
    shape = lambda *dims: jax.ShapeDtypeStruct(dims, f32)
    return pl.pallas_call(
        exchange,
        out_shape=(shape(4, 4, 2, 128, 256), shape(8, 256, 256), shape(2, 256, 256), shape(2, 512, 512), shape(2, 512, 256)),
        in_specs=[pl.BlockSpec(memory_space=pltpu.SMEM)] + [hbm] * 6,
        out_specs=(hbm, hbm, vm, hbm, hbm),
        scratch_shapes=[
            pltpu.VMEM((8, 256, 256), f32), pltpu.VMEM((4, 16, 2048), bf16), pltpu.VMEM((256, 2048), bf16),
            pltpu.VMEM((4, 4, 2, 128, 256), f32), pltpu.VMEM((8, 256, 256), f32),
            pltpu.VMEM((4, 4, 2, 128, 256), f32), pltpu.VMEM((8, 256, 256), f32),
            pltpu.VMEM((256, 256), f32), pltpu.VMEM((2, 256, 256), f32),
            pltpu.VMEM((4096, 256), f32), pltpu.VMEM((4096, 256), f32), pltpu.VMEM((4096, 256), f32),
            pltpu.VMEM((2, 512, 512), f32), pltpu.VMEM((2, 512, 512), f32), pltpu.VMEM((2, 512, 256), f32),
            dma((3,)), dma((3,)), dma((8,)), dma((8,)), dma((1,)), dma((1,)), dma((8,)), dma((8,)),
            dma((36,)), dma((36,)), dma((36,)), dma((36,)),
            dma((2,)), dma((16,)), dma((16,)), dma((16,)), dma((16,)), dma((16,)),
            dma((2,)), dma((16,)), dma((16,)), dma((16,)), dma((16,)), dma((16,)),
            dma((4,)), dma((6,)),
        ],
        compiler_params=pltpu.CompilerParams(collective_id=0, has_side_effects=True, vmem_limit_bytes=56 << 20),
        name="exchange",
    )(panel_rank, factor_inverse, panel_right, panel_left, left, right, probes)


def split2(a):
    hi = a.astype(bf16)
    return hi, (a - hi.astype(f32)).astype(bf16)


def mul(a, b):
    return jnp.dot(a, b, preferred_element_type=f32)


def dot3(a, b):
    a0, a1 = split2(a)
    b0, b1 = split2(b)
    return (mul(a0, b1) + mul(a1, b0)) + mul(a0, b0)


def dot6(a, b):
    a0, a1, a2 = split3(a)
    b0, b1, b2 = split3(b)
    small = mul(a1, b1) + mul(a0, b2) + mul(a2, b0)
    return (small + (mul(a0, b1) + mul(a1, b0))) + mul(a0, b0)


NB = 64


def factor_blocks(blocks):
    sub = lax.broadcasted_iota(jnp.int32, (8, 128), 0)
    lane = lax.broadcasted_iota(jnp.int32, (8, 128), 1)
    n = NB // 8
    all_rows = []
    for block in blocks:
        rows = []
        for g in range(n):
            unit = jnp.where(lane == sub + (NB + 8 * g), 1.0, 0.0)
            rows.append(jnp.concatenate([block[8 * g:8 * g + 8, :], unit[:, NB:]], axis=1))
        all_rows.append(rows)
    scales = [[None] * n for _ in blocks]
    for k in range(n):
        wide = [[[jnp.broadcast_to(rows[g][:, 8 * k + i:8 * k + i + 1], (8, 128)) for i in range(8)] if g >= k else None for g in range(n)] for rows in all_rows]
        pivots = [jnp.zeros((8, 128), f32) for _ in blocks]
        for i in range(8):
            for b, rows in enumerate(all_rows):
                w = wide[b]
                pivot = jnp.broadcast_to(w[k][i][i:i + 1, :], (8, 128))
                inverse = 1.0 / pivot
                pivots[b] = jnp.where(sub == i, pivot, pivots[b])
                row = jnp.broadcast_to(rows[k][i:i + 1, :], (8, 128))
                heads = [jnp.broadcast_to(w[k][j][i:i + 1, :], (8, 128)) for j in range(i + 1, 8)]
                for g in range(k, n):
                    factor = w[g][i] * inverse
                    if g == k:
                        factor = jnp.where(sub > i, factor, 0.0)
                    for j in range(i + 1, 8):
                        w[g][j] = w[g][j] - factor * heads[j - i - 1]
                    rows[g] = rows[g] - factor * row
        for b in range(len(blocks)):
            scales[b][k] = lax.rsqrt(pivots[b])
    return [jnp.concatenate([rows[g] * scales[b][g] for g in range(n)], axis=0)[:, NB:] for b, rows in enumerate(all_rows)]


def solve_rows(g_refs, c_refs):
    count = len(g_refs)
    for k in range(256 // NB):
        lo, hi = k * NB, (k + 1) * NB
        inverses = factor_blocks([g[lo:hi, lo:hi] for g in g_refs])
        for b in range(count):
            g, c = g_refs[b], c_refs[b]
            if hi < 256:
                gu = dot6(inverses[b], g[lo:hi, hi:])
            cu = dot6(inverses[b], c[lo:hi, :])
            c[lo:hi, :] = cu
            if hi < 256:
                gt = gu.T
                g[hi:, hi:] -= dot6(gt, gu)
                c[hi:, :] -= dot6(gt, cu)


CHUNK = 512


def tiles_kernel(rank_ref, left, right, ug, uq, core_in, hh_in, cc_in, out_left, out_right,
                 xu, xv, xg, xq, yl, yr, core, hh, cc, gg, ct, ds0, ds1, es0, es1, in_sem, out_sem):
    order = 2048
    copies = [pltpu.make_async_copy(src, dst, in_sem.at[i]) for i, (src, dst) in enumerate((
        (core_in, core), (cc_in, cc), (hh_in, hh), (left, xu), (ug, xg), (right, xv), (uq, xq)))]
    for c in copies:
        c.start()
    columns = lax.broadcasted_iota(jnp.int32, (256, 256), 1)
    rows_at = lax.broadcasted_iota(jnp.int32, (256, 256), 0)
    for c in copies[:3]:
        c.wait()
    for t in range(2):
        keep = columns < rank_ref[t]
        scale = 1.0 / order
        c1 = jnp.where(jnp.logical_and(keep, rows_at < rank_ref[t]), cc[t, :256], 0.0) * scale
        pp = jnp.where(keep, cc[t, 256:], 0.0) * -scale
        c2 = dot6(core[t], pp)
        c = jnp.concatenate([c1, c2], axis=0)
        ct[t] = c.T
        hc = dot6(hh[t], c)
        unit = jnp.where(jnp.logical_and(columns == rows_at, jnp.logical_not(keep)), 1.0, 0.0)
        gg[t] = dot6(ct[t], hc) + unit
    solve_rows([gg.at[0], gg.at[1]], [ct.at[0], ct.at[1]])
    for c in copies[3:]:
        c.wait()
    stores = []
    for t in range(2):
        rank = rank_ref[t]
        d = (ct[t] * math.sqrt(order)).T
        d0, d1 = split2(d)
        ds0[t], ds1[t] = d0, d1
        h0, h1 = split2(hh[t])
        hd = (mul(h0, d1) + mul(h1, d0)) + mul(h0, d0)
        e1 = jnp.where(rows_at < rank, hd[:256], 0.0) * (1.0 / order)
        e2 = dot3(core[t].T, hd[256:]) * (-1.0 / order)
        es0[t], es1[t] = split2(jnp.concatenate([e1, e2], axis=0))

        @pl.loop(0, order // CHUNK)
        def _(j):
            at = pl.ds(pl.multiple_of(t * order + j * CHUNK, CHUNK), CHUNK)
            x0, x1 = split2(jnp.concatenate([xu[at, :], xg[at, :]], axis=1))
            yl[at, :] = (mul(x0, ds1[t]) + mul(x1, ds0[t])) + mul(x0, ds0[t])

        rows = pl.ds(t * order, order)
        stores.append(pltpu.make_async_copy(yl.at[rows], out_left.at[rows], out_sem.at[2 * t]))
        stores[-1].start()

        @pl.loop(0, order // CHUNK)
        def _(j):
            at = pl.ds(pl.multiple_of(t * order + j * CHUNK, CHUNK), CHUNK)
            atq = pl.ds(pl.multiple_of(j * CHUNK, CHUNK), CHUNK)
            x0, x1 = split2(jnp.concatenate([xv[at, :], xq[atq, :]], axis=1))
            yr[at, :] = (mul(x0, es1[t]) + mul(x1, es0[t])) + mul(x0, es0[t])

        stores.append(pltpu.make_async_copy(yr.at[rows], out_right.at[rows], out_sem.at[2 * t + 1]))
        stores[-1].start()
    for store in stores:
        store.wait()


def run_tiles(trail_rank, left, right, ug, uq, core, hh, cc):
    hbm = pl.BlockSpec(memory_space=pl.ANY)
    big = pltpu.VMEM((4096, 256), f32)
    return pl.pallas_call(
        tiles_kernel,
        out_shape=(jax.ShapeDtypeStruct((4096, 256), f32),) * 2,
        in_specs=[pl.BlockSpec(memory_space=pltpu.SMEM)] + [hbm] * 7,
        out_specs=(hbm, hbm),
        scratch_shapes=[big, big, big, pltpu.VMEM((2048, 256), f32), big, big, pltpu.VMEM((2, 256, 256), f32),
                        pltpu.VMEM((2, 512, 512), f32), pltpu.VMEM((2, 512, 256), f32),
                        pltpu.VMEM((2, 256, 256), f32), pltpu.VMEM((2, 256, 512), f32)]
        + [pltpu.VMEM((2, 512, 256), bf16)] * 4
        + [pltpu.SemaphoreType.DMA((7,)), pltpu.SemaphoreType.DMA((4,))],
        compiler_params=pltpu.CompilerParams(vmem_limit_bytes=56 << 20),
        name="tiles",
    )(trail_rank, left, right, ug, uq, core, hh, cc)


def shards(factor_inverse, panel_left, panel_right, panel_rank, left, right, probes, trail_rank):
    ug, uq, core, hh, cc = run_exchange(panel_rank, factor_inverse, panel_right, panel_left, left, right, probes)
    ug, uq = ug.reshape(4096, 256), uq.reshape(2048, 256)
    return run_tiles(trail_rank.reshape(-1), left, right, ug, uq, core, hh, cc)


def solution(mesh):
    return jax.shard_map(
        shards,
        mesh=mesh,
        in_specs=(
            P(("row", "col"), None),
            P(("row", "col"), None),
            P(("row", "col"), None),
            P("row"),
            P("row", "col"),
            P("row", "col"),
            P("row", "col"),
            P("row", "col"),
        ),
        out_specs=(P("row", "col"), P("row", "col")),
        check_vma=False,
    )
```

```python
import functools
import math

import jax
import jax.numpy as jnp
from jax import lax
from jax.experimental import pallas as pl
from jax.experimental.pallas import tpu as pltpu
from jax.sharding import PartitionSpec as P

MESH = pl.DeviceIdType.MESH
f32, bf16 = jnp.float32, jnp.bfloat16


def split3(a):
    hi = a.astype(bf16)
    rest = a - hi.astype(f32)
    mid = rest.astype(bf16)
    return hi, mid, (rest - mid.astype(f32)).astype(bf16)


def exchange(rank_ref, inv_ref, right_ref, left_ref, tiles_u, tiles_v, tiles_o, ug_out, uq_out, core_out, hh_out, cc_out,
             rb, l1, lb, wg, wq, ug, uq, acc, rtmp, xu, xv, xo, hh, hl, cc,
             l1_s, l1_r, l_s, l_r, lf_s, lf_r, r_s, r_r, w_s, w_r, u_s, u_r,
             wo_s, wo_r, wz_s, wz_r, wc_s, wc_r, uo_s, uo_r, uz_s, uz_r, uc_s, uc_r, loc, load):
    row, col = lax.axis_index("row"), lax.axis_index("col")
    z, core = row // 2, row % 2
    x, y = col // 4, col % 4
    xp, xm, x2 = (x + 1) % 4, (x + 3) % 4, (x + 2) % 4
    yp, ym, y2 = (y + 1) % 4, (y + 3) % 4, (y + 2) % 4
    cx = x % 2
    chunk = cx * 4 + y
    sibling = (z * 2 + (1 - core), col)

    def at(xx, yy):
        return (row, xx * 4 + yy)

    pair = at(x + 1 - 2 * cx, y)
    up, down = ((z + 1) % 4 * 2 + core, col), ((z + 3) % 4 * 2 + core, col)

    opposite = ((z + 2) % 4 * 2 + core, col)
    home = ((z + chunk // 2) % 4 * 2 + core, 2 * row + x // 2)
    is_home = jnp.logical_and(chunk // 2 == 0, home[1] == col)
    home_half = col % 2
    dz = (z - x + 4) % 4
    home_core = y // 2
    on_home_core = core == home_core

    own_loads = [pltpu.make_async_copy(src, dst, load.at[i]) for i, (src, dst) in enumerate((
        (right_ref, rtmp.at[0]), (left_ref, rtmp.at[1]), (inv_ref, l1.at[z])))]
    tile_loads = [pltpu.make_async_copy(src, dst, load.at[3 + i]) for i, (src, dst) in enumerate((
        (tiles_v, xv), (tiles_o, xo), (tiles_u, xu)))]
    for c in own_loads + tile_loads:
        c.start()

    bar = pltpu.get_barrier_semaphore()

    def greet(who, skip=None):
        if skip is None:
            pl.semaphore_signal(bar, inc=1, device_id=who, device_id_type=MESH)
        else:
            @pl.when(jnp.logical_not(skip))
            def _():
                pl.semaphore_signal(bar, inc=1, device_id=who, device_id_type=MESH)

    for who in (at(xp, y), at(xm, y), at(x, yp), at(x, ym), up, down, opposite, sibling):
        greet(who)
    for j in range(8):
        src = (z * 2 + chunk % 2, core * 8 + j)
        greet(src, jnp.logical_and(src[0] == row, src[1] == col))

    @pl.when(on_home_core)
    def _():
        for j in range(2):
            src = (2 * x + core, home_half * 8 + 2 * dz + j)
            greet(src, jnp.logical_and(src[0] == row, src[1] == col))

    l_self = jnp.logical_and(chunk % 2 == core, x // 2 == core)

    for c in own_loads:
        c.wait()
    rank = jnp.where(x // 2 == 0, rank_ref[0], rank_ref[1])
    keep = lax.broadcasted_iota(jnp.int32, (256, 256), 1) < rank
    rb[chunk] = jnp.where(keep, rtmp[0], 0.0)
    ug[x, y] = jnp.where(keep, rtmp[1], 0.0).reshape(2, 128, 256)
    pl.semaphore_wait(bar, 17 - jnp.where(l_self, 1, 0) - jnp.where(is_home, 1, 0))

    def remote(src, dst, ss, rs, who):
        return pltpu.make_async_remote_copy(
            src_ref=src, dst_ref=dst, send_sem=ss, recv_sem=rs, device_id=who, device_id_type=MESH)

    def send(buf, idx, ss, rs, i, who):
        remote(buf.at[idx], buf.at[idx], ss.at[i], rs.at[i], who).start()

    def arrive(buf, idx, rs, i):
        pltpu.make_async_copy(buf.at[idx], buf.at[idx], rs.at[i]).wait()

    def sent(buf, idx, ss, i):
        pltpu.make_async_copy(buf.at[idx], buf.at[idx], ss.at[i]).wait()

    own_c, pair_c = cx * 4, (1 - cx) * 4
    lo_half, hi_half = pl.ds(0, 128), pl.ds(128, 128)

    for i, who in enumerate((up, down, opposite)):
        remote(l1.at[z], l1.at[z], l1_s.at[i], l1_r.at[i], who).start()

    send(rb, chunk, r_s, r_r, 0, at(x, yp))
    send(rb, chunk, r_s, r_r, 1, at(x, ym))
    send(rb, chunk, r_s, r_r, 2, pair)

    def l_second():
        arrive(l1, (z + 3) % 4, l1_r, 0)
        arrive(l1, (z + 1) % 4, l1_r, 1)
        arrive(l1, (z + 2) % 4, l1_r, 2)
        for dzz in range(4):
            zz = (z + dzz) % 4
            c = 2 * zz + core
            for dx in range(2):
                who = (z * 2 + x // 2, (c // 4 + 2 * dx) * 4 + c % 4)
                me = jnp.logical_and(who[0] == row, who[1] == col)
                src = l1.at[zz]

                @pl.when(jnp.logical_not(me))
                def _():
                    remote(src, lb.at[l_piece], l_s.at[dzz * 2 + dx], l_r.at[j_own], who).start()

                @pl.when(me)
                def _():
                    pltpu.make_async_copy(src, lb.at[l_piece], l_r.at[j_own]).start()

    def l_finish():
        for i in range(3):
            pltpu.make_async_copy(l1.at[0], l1.at[0], l1_s.at[i]).wait()
        for dzz in range(4):
            c = 2 * ((z + dzz) % 4) + core
            for dx in range(2):
                me = jnp.logical_and(z * 2 + x // 2 == row, (c // 4 + 2 * dx) * 4 + c % 4 == col)

                @pl.when(jnp.logical_not(me))
                def _():
                    pltpu.make_async_copy(l1.at[0], l1.at[0], l_s.at[dzz * 2 + dx]).wait()

    l_piece = pl.ds(pl.multiple_of(col * 16, 16), 16)
    j_own = col % 8

    def gather(buf, ss, rs):
        done = []

        def snd(idx, i, who):
            send(buf, idx, ss, rs, i, who)
            done.append((idx, i))

        def arr(idx, i):
            arrive(buf, idx, rs, i)

        q0, q1 = pl.ds(0, 64), pl.ds(64, 64)
        XP, XM, YP, YM = at(xp, y), at(xm, y), at(x, yp), at(x, ym)

        def s0():
            snd((x, y), 0, YP)
            snd((x, y), 1, YM)
            snd((x, y), 2, XP)
            snd((x, y), 3, XM)

        def s1():
            arr((x, ym), 0)
            snd((x, ym, 0, q0), 4, YP)
            snd((x, ym, 0), 5, XP)
            snd((x, ym, 0), 6, XM)
            snd((x, ym, 1, q0), 28, YP)

        def s2():
            arr((xm, y), 2)
            snd((xm, y, 1, q0), 20, XP)
            snd((xm, y, 1), 21, YP)
            snd((xm, y, 1), 22, YM)
            snd((xm, y, 0, q0), 12, XP)

        def s3():
            arr((x, yp), 1)
            snd((x, yp, 0, q1), 7, YM)
            snd((x, yp, 0), 8, XP)
            snd((x, yp, 0), 9, XM)
            snd((x, yp, 1, q1), 29, YM)

        def s4():
            arr((xp, y), 3)
            snd((xp, y, 1, q1), 23, XM)
            snd((xp, y, 1), 24, YP)
            snd((xp, y, 1), 25, YM)
            snd((xp, y, 0, q1), 13, XM)

        def s5():
            arr((x, y2, 0, q0), 4)
            arr((x, y2, 0, q1), 7)
            snd((x, y2, 0), 10, XP)
            snd((x, y2, 0), 11, XM)

        def s6():
            arr((x2, y, 1, q0), 20)
            arr((x2, y, 1, q1), 23)
            snd((x2, y, 1), 26, YP)
            snd((x2, y, 1), 27, YM)

        def s7():
            arr((xm, ym, 0), 5)
            snd((xm, ym, 0, q0), 14, XP)
            arr((xp, ym, 0), 6)
            snd((xp, ym, 0, q1), 15, XM)
            arr((xm, ym, 1), 21)
            snd((xm, ym, 1, q0), 30, YP)
            arr((xm, yp, 1), 22)
            snd((xm, yp, 1, q1), 31, YM)

        def s8():
            arr((xm, yp, 0), 8)
            snd((xm, yp, 0, q0), 16, XP)
            arr((xp, yp, 0), 9)
            snd((xp, yp, 0, q1), 17, XM)
            arr((xp, ym, 1), 24)
            snd((xp, ym, 1, q0), 32, YP)
            arr((xp, yp, 1), 25)
            snd((xp, yp, 1, q1), 33, YM)

        def s9():
            arr((xm, y2, 0), 10)
            snd((xm, y2, 0, q0), 18, XP)
            arr((xp, y2, 0), 11)
            snd((xp, y2, 0, q1), 19, XM)
            arr((x2, ym, 1), 26)
            snd((x2, ym, 1, q0), 34, YP)
            arr((x2, yp, 1), 27)
            snd((x2, yp, 1, q1), 35, YM)

        def s10():
            arr((x2, y, 0, q0), 12)
            arr((x2, y, 0, q1), 13)
            arr((x, y2, 1, q0), 28)
            arr((x, y2, 1, q1), 29)
            arr((x2, ym, 0, q0), 14)
            arr((x2, ym, 0, q1), 15)
            arr((xm, y2, 1, q0), 30)
            arr((xm, y2, 1, q1), 31)

        def s11():
            arr((x2, yp, 0, q0), 16)
            arr((x2, yp, 0, q1), 17)
            arr((xp, y2, 1, q0), 32)
            arr((xp, y2, 1, q1), 33)
            arr((x2, y2, 0, q0), 18)
            arr((x2, y2, 0, q1), 19)
            arr((x2, y2, 1, q0), 34)
            arr((x2, y2, 1, q1), 35)

        def finish():
            for idx, i in done:
                sent(buf, idx, ss, i)

        return [s0, s1, s2, s3, s4, s5, s6, s7, s8, s9, s10, s11], finish

    halves = [pl.ds(0, 128), pl.ds(128, 128)]

    def to_home(buf, qbuf, os, orr):
        for hh in range(2):
            @pl.when(jnp.logical_not(is_home))
            def _():
                remote(buf.at[x, y, hh], qbuf.at[chunk, halves[hh]], os.at[hh], orr.at[2 * chunk + hh], home).start()

            @pl.when(is_home)
            def _():
                pltpu.make_async_copy(buf.at[x, y, hh], qbuf.at[chunk, halves[hh]], orr.at[2 * chunk + hh]).start()

    def to_home_finish(buf, os):
        for hh in range(2):
            @pl.when(jnp.logical_not(is_home))
            def _():
                pltpu.make_async_copy(buf.at[x, y, hh], buf.at[x, y, hh], os.at[hh]).wait()

    def ring(qbuf, orr, zs, zr, cs, cr):
        idx_of = lambda k: (k // 2, halves[k % 2])
        carries = lambda k: core == (home_core + k) % 2
        onward = lambda k: up if (k // 2) % 2 == 0 else down
        off = lambda k: (dz + 4 - k // 4) % 4
        hop_of = lambda k: off(k) if (k // 2) % 2 == 0 else (4 - off(k)) % 4
        at_source = lambda k: jnp.logical_and(off(k) == 0, on_home_core)

        def src(k):
            idx = idx_of(k)

            @pl.when(at_source(k))
            def _():
                arrive(qbuf, idx, orr, k)
                if k % 2 == 0:
                    send(qbuf, idx, zs, zr, k, onward(k))
                send(qbuf, idx, cs, cr, k, sibling)

            if k % 2 == 1:
                @pl.when(jnp.logical_and(off(k) == 0, jnp.logical_not(on_home_core)))
                def _():
                    arrive(qbuf, idx, cr, k)
                    send(qbuf, idx, zs, zr, k, onward(k))

        def hop(number, k):
            idx = idx_of(k)

            @pl.when(jnp.logical_and(hop_of(k) == number, carries(k)))
            def _():
                arrive(qbuf, idx, zr, k)
                if number < 3:
                    send(qbuf, idx, zs, zr, k, onward(k))
                send(qbuf, idx, cs, cr, k, sibling)

        def end(k):
            waits = jnp.logical_and(jnp.logical_not(carries(k)), jnp.logical_not(at_source(k)))

            @pl.when(waits)
            def _():
                arrive(qbuf, idx_of(k), cr, k)

        def finish():
            for k in range(16):
                idx = idx_of(k)

                @pl.when(jnp.logical_and(carries(k), hop_of(k) != 3))
                def _():
                    sent(qbuf, idx, zs, k)

                @pl.when(jnp.logical_or(at_source(k), jnp.logical_and(off(k) != 0, carries(k))))
                def _():
                    sent(qbuf, idx, cs, k)

        return src, hop, end, finish

    u_steps, u_finish = gather(ug, u_s, u_r)
    w_steps, w_finish = gather(wg, w_s, w_r)
    uz_src, uz_hop, uz_end, uz_finish = ring(uq, uo_r, uz_s, uz_r, uc_s, uc_r)
    wz_src, wz_hop, wz_end, wz_finish = ring(wq, wo_r, wz_s, wz_r, wc_s, wc_r)

    def pick(options, n):
        value = options[0]
        for i in range(1, len(options)):
            value = jnp.where(n == i, options[i], value)
        return value

    def right_probe(t):
        cc[t, :256] = jnp.zeros((256, 256), f32)

        @pl.loop(0, 4)
        def _(j):
            rows = pl.ds(pl.multiple_of(t * 2048 + j * 512, 512), 512)
            cc[t, :256] += dot6(xv[rows, :].T, xo[rows, :])

    def panel_probe(t):
        cc[t, 256:] = jnp.zeros((256, 256), f32)

        @pl.loop(0, 4)
        def _(j):
            rows = pl.ds(pl.multiple_of(t * 2048 + j * 512, 512), 512)
            cc[t, 256:] += dot6(uq[pl.ds(2 * j, 2)].reshape(512, 256).T, xo[rows, :])

    def cross(t):
        acc[...] = jnp.zeros_like(acc)

        @pl.loop(0, 4)
        def _(i):
            w = wg[2 * t + i // 2, pl.ds((i % 2) * 2, 2)].reshape(512, 256)
            acc[...] += dot6(w.T, wq[pl.ds(2 * i, 2)].reshape(512, 256))

        core_out[t] = acc[...] * (1.0 / 2048)

    def squares(places):
        @pl.loop(0, len(places))
        def _(n):
            px, py = pick([p[0] for p in places], n), pick([p[1] for p in places], n)
            rows = pl.ds(pl.multiple_of((px * 4 + py) * 256, 256), 256)
            t = px // 2
            x0, x1 = split2(jnp.concatenate([xu[rows, :], ug[px, py].reshape(256, 256)], axis=1))
            x0t = x0.T
            hh[t] += mul(x0t, x0)
            hl[t] += mul(x0t, x1)

    U = lambda *ks: [u_steps[k]() for k in ks]
    W = lambda *ks: [w_steps[k]() for k in ks]
    every = lambda fn, ks=range(16): [fn(k) for k in ks]

    to_home(ug, uq, uo_s, uo_r)
    l_second()
    tile_loads[0].wait()
    tile_loads[1].wait()
    right_probe(0)
    arrive(rb, own_c + ym, r_r, 0)
    send(rb, (own_c + ym, lo_half), r_s, r_r, 5, at(x, yp))
    arrive(rb, own_c + yp, r_r, 1)
    send(rb, (own_c + yp, hi_half), r_s, r_r, 6, at(x, ym))
    arrive(rb, pair_c + y, r_r, 2)
    send(rb, pair_c + y, r_s, r_r, 3, at(x, yp))
    send(rb, pair_c + y, r_s, r_r, 4, at(x, ym))
    arrive(rb, (own_c + y2, lo_half), r_r, 5)
    arrive(rb, (own_c + y2, hi_half), r_r, 6)
    send(rb, own_c + y2, r_s, r_r, 7, pair)
    for j in range(8):
        arrive(lb, pl.ds(pl.multiple_of(core * 128 + j * 16, 16), 16), l_r, j)
    my_half = pl.ds(pl.multiple_of(core * 128, 128), 128)
    other_half = pl.ds(pl.multiple_of(128 - core * 128, 128), 128)
    send(lb, my_half, lf_s, lf_r, 0, sibling)
    U(0)
    right_probe(1)
    tile_loads[2].wait()
    hh[...] = jnp.zeros_like(hh)
    hl[...] = jnp.zeros_like(hl)
    arrive(rb, pair_c + ym, r_r, 3)
    arrive(rb, pair_c + yp, r_r, 4)
    arrive(rb, pair_c + y2, r_r, 7)
    arrive(lb, other_half, lf_r, 0)
    acc[...] = jnp.zeros_like(acc)

    @pl.loop(0, 8)
    def _(j):
        low = lb[:, pl.ds(pl.multiple_of(j * 256, 256), 256)]
        h0, h1, h2 = split3(rb[j])
        acc[...] += (mul(low, h2) + mul(low, h1)) + mul(low, h0)

    wg[x, y] = acc[...].reshape(2, 128, 256)
    W(0)
    to_home(wg, wq, wo_s, wo_r)
    interleaved = range(16)
    hop = lambda fn, number: [fn(number, k) for k in interleaved]
    every(uz_src, interleaved)
    W(1, 2, 3, 4)
    every(wz_src, interleaved)
    hop(uz_hop, 1)
    W(5, 6, 7, 8)
    hop(uz_hop, 2)
    hop(wz_hop, 1)
    W(9, 10)
    U(1, 2, 3, 4)
    hop(uz_hop, 3)
    hop(wz_hop, 2)
    W(11)
    every(uz_end)
    panel_probe(0)
    U(5, 6)
    hop(wz_hop, 3)
    squares([(x, y), (x, ym), (xm, y), (x, yp), (xp, y)])
    U(7, 8)
    panel_probe(1)
    every(wz_end)
    cross(0)
    U(9)
    cross(1)
    U(10)
    squares([(xm, ym), (xp, ym), (xm, yp), (xp, yp), (x2, y), (x, y2), (x2, ym), (xm, y2)])
    U(11)
    outs = [pltpu.make_async_copy(src, dst, loc.at[i]) for i, (src, dst) in enumerate((
        (ug, ug_out), (uq, uq_out), (cc, cc_out), (hh, hh_out)))]
    for c in outs[:3]:
        c.start()
    squares([(x2, yp), (xp, y2), (x2, y2)])
    for t in range(2):
        hh[t] += hl[t] + hl[t].T
    outs[3].start()
    sent(rb, chunk, r_s, 0)
    sent(rb, chunk, r_s, 1)
    sent(rb, chunk, r_s, 2)
    sent(rb, pair_c + y, r_s, 3)
    sent(rb, pair_c + y, r_s, 4)
    sent(rb, (own_c + ym, lo_half), r_s, 5)
    sent(rb, (own_c + yp, hi_half), r_s, 6)
    sent(rb, own_c + y2, r_s, 7)
    sent(lb, my_half, lf_s, 0)
    l_finish()

    u_finish()
    w_finish()
    uz_finish()
    to_home_finish(ug, uo_s)
    wz_finish()
    to_home_finish(wg, wo_s)
    for c in outs:
        c.wait()


def run_exchange(panel_rank, factor_inverse, panel_right, panel_left, left, right, probes):
    dma = pltpu.SemaphoreType.DMA
    vm = pl.BlockSpec(memory_space=pltpu.VMEM)
    hbm = pl.BlockSpec(memory_space=pl.ANY)
    shape = lambda *dims: jax.ShapeDtypeStruct(dims, f32)
    return pl.pallas_call(
        exchange,
        out_shape=(shape(4, 4, 2, 128, 256), shape(8, 256, 256), shape(2, 256, 256), shape(2, 512, 512), shape(2, 512, 256)),
        in_specs=[pl.BlockSpec(memory_space=pltpu.SMEM)] + [hbm] * 6,
        out_specs=(hbm, hbm, vm, hbm, hbm),
        scratch_shapes=[
            pltpu.VMEM((8, 256, 256), f32), pltpu.VMEM((4, 16, 2048), bf16), pltpu.VMEM((256, 2048), bf16),
            pltpu.VMEM((4, 4, 2, 128, 256), f32), pltpu.VMEM((8, 256, 256), f32),
            pltpu.VMEM((4, 4, 2, 128, 256), f32), pltpu.VMEM((8, 256, 256), f32),
            pltpu.VMEM((256, 256), f32), pltpu.VMEM((2, 256, 256), f32),
            pltpu.VMEM((4096, 256), f32), pltpu.VMEM((4096, 256), f32), pltpu.VMEM((4096, 256), f32),
            pltpu.VMEM((2, 512, 512), f32), pltpu.VMEM((2, 512, 512), f32), pltpu.VMEM((2, 512, 256), f32),
            dma((3,)), dma((3,)), dma((8,)), dma((8,)), dma((1,)), dma((1,)), dma((8,)), dma((8,)),
            dma((36,)), dma((36,)), dma((36,)), dma((36,)),
            dma((2,)), dma((16,)), dma((16,)), dma((16,)), dma((16,)), dma((16,)),
            dma((2,)), dma((16,)), dma((16,)), dma((16,)), dma((16,)), dma((16,)),
            dma((4,)), dma((6,)),
        ],
        compiler_params=pltpu.CompilerParams(collective_id=0, has_side_effects=True, vmem_limit_bytes=56 << 20),
        name="exchange",
    )(panel_rank, factor_inverse, panel_right, panel_left, left, right, probes)


def split2(a):
    hi = a.astype(bf16)
    return hi, (a - hi.astype(f32)).astype(bf16)


def mul(a, b):
    return jnp.dot(a, b, preferred_element_type=f32)


def dot3(a, b):
    a0, a1 = split2(a)
    b0, b1 = split2(b)
    return (mul(a0, b1) + mul(a1, b0)) + mul(a0, b0)


def dot6(a, b):
    a0, a1, a2 = split3(a)
    b0, b1, b2 = split3(b)
    small = mul(a1, b1) + mul(a0, b2) + mul(a2, b0)
    return (small + (mul(a0, b1) + mul(a1, b0))) + mul(a0, b0)


NB = 64


def factor_blocks(blocks):
    sub = lax.broadcasted_iota(jnp.int32, (8, 128), 0)
    lane = lax.broadcasted_iota(jnp.int32, (8, 128), 1)
    n = NB // 8
    all_rows = []
    for block in blocks:
        rows = []
        for g in range(n):
            unit = jnp.where(lane == sub + (NB + 8 * g), 1.0, 0.0)
            rows.append(jnp.concatenate([block[8 * g:8 * g + 8, :], unit[:, NB:]], axis=1))
        all_rows.append(rows)
    scales = [[None] * n for _ in blocks]
    for k in range(n):
        wide = [[[jnp.broadcast_to(rows[g][:, 8 * k + i:8 * k + i + 1], (8, 128)) for i in range(8)] if g >= k else None for g in range(n)] for rows in all_rows]
        pivots = [jnp.zeros((8, 128), f32) for _ in blocks]
        for i in range(8):
            for b, rows in enumerate(all_rows):
                w = wide[b]
                pivot = jnp.broadcast_to(w[k][i][i:i + 1, :], (8, 128))
                inverse = 1.0 / pivot
                pivots[b] = jnp.where(sub == i, pivot, pivots[b])
                row = jnp.broadcast_to(rows[k][i:i + 1, :], (8, 128))
                heads = [jnp.broadcast_to(w[k][j][i:i + 1, :], (8, 128)) for j in range(i + 1, 8)]
                for g in range(k, n):
                    factor = w[g][i] * inverse
                    if g == k:
                        factor = jnp.where(sub > i, factor, 0.0)
                    for j in range(i + 1, 8):
                        w[g][j] = w[g][j] - factor * heads[j - i - 1]
                    rows[g] = rows[g] - factor * row
        for b in range(len(blocks)):
            scales[b][k] = lax.rsqrt(pivots[b])
    return [jnp.concatenate([rows[g] * scales[b][g] for g in range(n)], axis=0)[:, NB:] for b, rows in enumerate(all_rows)]


def solve_rows(g_refs, c_refs):
    count = len(g_refs)
    for k in range(256 // NB):
        lo, hi = k * NB, (k + 1) * NB
        inverses = factor_blocks([g[lo:hi, lo:hi] for g in g_refs])
        for b in range(count):
            g, c = g_refs[b], c_refs[b]
            if hi < 256:
                gu = dot6(inverses[b], g[lo:hi, hi:])
            cu = dot6(inverses[b], c[lo:hi, :])
            c[lo:hi, :] = cu
            if hi < 256:
                gt = gu.T
                g[hi:, hi:] -= dot6(gt, gu)
                c[hi:, :] -= dot6(gt, cu)


CHUNK = 512


def tiles_kernel(rank_ref, left, right, ug, uq, core_in, hh_in, cc_in, out_left, out_right,
                 xu, xv, xg, xq, yl, yr, core, hh, cc, gg, ct, ds0, ds1, es0, es1, in_sem, out_sem):
    order = 2048
    copies = [pltpu.make_async_copy(src, dst, in_sem.at[i]) for i, (src, dst) in enumerate((
        (core_in, core), (cc_in, cc), (hh_in, hh), (left, xu), (ug, xg), (right, xv), (uq, xq)))]
    for c in copies:
        c.start()
    columns = lax.broadcasted_iota(jnp.int32, (256, 256), 1)
    rows_at = lax.broadcasted_iota(jnp.int32, (256, 256), 0)
    for c in copies[:3]:
        c.wait()
    for t in range(2):
        keep = columns < rank_ref[t]
        scale = 1.0 / order
        c1 = jnp.where(jnp.logical_and(keep, rows_at < rank_ref[t]), cc[t, :256], 0.0) * scale
        pp = jnp.where(keep, cc[t, 256:], 0.0) * -scale
        c2 = dot6(core[t], pp)
        c = jnp.concatenate([c1, c2], axis=0)
        ct[t] = c.T
        hc = dot6(hh[t], c)
        unit = jnp.where(jnp.logical_and(columns == rows_at, jnp.logical_not(keep)), 1.0, 0.0)
        gg[t] = dot6(ct[t], hc) + unit
    solve_rows([gg.at[0], gg.at[1]], [ct.at[0], ct.at[1]])
    for c in copies[3:]:
        c.wait()
    stores = []
    for t in range(2):
        rank = rank_ref[t]
        d = (ct[t] * math.sqrt(order)).T
        d0, d1 = split2(d)
        ds0[t], ds1[t] = d0, d1
        h0, h1 = split2(hh[t])
        hd = (mul(h0, d1) + mul(h1, d0)) + mul(h0, d0)
        e1 = jnp.where(rows_at < rank, hd[:256], 0.0) * (1.0 / order)
        e2 = dot3(core[t].T, hd[256:]) * (-1.0 / order)
        es0[t], es1[t] = split2(jnp.concatenate([e1, e2], axis=0))

        @pl.loop(0, order // CHUNK)
        def _(j):
            at = pl.ds(pl.multiple_of(t * order + j * CHUNK, CHUNK), CHUNK)
            x0, x1 = split2(jnp.concatenate([xu[at, :], xg[at, :]], axis=1))
            yl[at, :] = (mul(x0, ds1[t]) + mul(x1, ds0[t])) + mul(x0, ds0[t])

        rows = pl.ds(t * order, order)
        stores.append(pltpu.make_async_copy(yl.at[rows], out_left.at[rows], out_sem.at[2 * t]))
        stores[-1].start()

        @pl.loop(0, order // CHUNK)
        def _(j):
            at = pl.ds(pl.multiple_of(t * order + j * CHUNK, CHUNK), CHUNK)
            atq = pl.ds(pl.multiple_of(j * CHUNK, CHUNK), CHUNK)
            x0, x1 = split2(jnp.concatenate([xv[at, :], xq[atq, :]], axis=1))
            yr[at, :] = (mul(x0, es1[t]) + mul(x1, es0[t])) + mul(x0, es0[t])

        stores.append(pltpu.make_async_copy(yr.at[rows], out_right.at[rows], out_sem.at[2 * t + 1]))
        stores[-1].start()
    for store in stores:
        store.wait()


def run_tiles(trail_rank, left, right, ug, uq, core, hh, cc):
    hbm = pl.BlockSpec(memory_space=pl.ANY)
    big = pltpu.VMEM((4096, 256), f32)
    return pl.pallas_call(
        tiles_kernel,
        out_shape=(jax.ShapeDtypeStruct((4096, 256), f32),) * 2,
        in_specs=[pl.BlockSpec(memory_space=pltpu.SMEM)] + [hbm] * 7,
        out_specs=(hbm, hbm),
        scratch_shapes=[big, big, big, pltpu.VMEM((2048, 256), f32), big, big, pltpu.VMEM((2, 256, 256), f32),
                        pltpu.VMEM((2, 512, 512), f32), pltpu.VMEM((2, 512, 256), f32),
                        pltpu.VMEM((2, 256, 256), f32), pltpu.VMEM((2, 256, 512), f32)]
        + [pltpu.VMEM((2, 512, 256), bf16)] * 4
        + [pltpu.SemaphoreType.DMA((7,)), pltpu.SemaphoreType.DMA((4,))],
        compiler_params=pltpu.CompilerParams(vmem_limit_bytes=56 << 20),
        name="tiles",
    )(trail_rank, left, right, ug, uq, core, hh, cc)


def shards(factor_inverse, panel_left, panel_right, panel_rank, left, right, probes, trail_rank):
    ug, uq, core, hh, cc = run_exchange(panel_rank, factor_inverse, panel_right, panel_left, left, right, probes)
    ug, uq = ug.reshape(4096, 256), uq.reshape(2048, 256)
    return run_tiles(trail_rank.reshape(-1), left, right, ug, uq, core, hh, cc)


def solution(mesh):
    return jax.shard_map(
        shards,
        mesh=mesh,
        in_specs=(
            P(("row", "col"), None),
            P(("row", "col"), None),
            P(("row", "col"), None),
            P("row"),
            P("row", "col"),
            P("row", "col"),
            P("row", "col"),
            P("row", "col"),
        ),
        out_specs=(P("row", "col"), P("row", "col")),
        check_vma=False,
    )
```

```python
import functools
import math

import jax
import jax.numpy as jnp
from jax import lax
from jax.experimental import pallas as pl
from jax.experimental.pallas import tpu as pltpu
from jax.sharding import PartitionSpec as P

MESH = pl.DeviceIdType.MESH
f32, bf16 = jnp.float32, jnp.bfloat16


def split3(a):
    hi = a.astype(bf16)
    rest = a - hi.astype(f32)
    mid = rest.astype(bf16)
    return hi, mid, (rest - mid.astype(f32)).astype(bf16)


def exchange(rank_ref, inv_ref, right_ref, left_ref, tiles_u, tiles_v, tiles_o, ug_out, uq_out, core_out, hh_out, cc_out,
             rb, l1, lb, wg, wq, ug, uq, acc, rtmp, xu, xv, xo, hh, hl, cc,
             l1_s, l1_r, l_s, l_r, lf_s, lf_r, r_s, r_r, w_s, w_r, u_s, u_r,
             wo_s, wo_r, wz_s, wz_r, wc_s, wc_r, uo_s, uo_r, uz_s, uz_r, uc_s, uc_r, loc, load):
    row, col = lax.axis_index("row"), lax.axis_index("col")
    z, core = row // 2, row % 2
    x, y = col // 4, col % 4
    xp, xm, x2 = (x + 1) % 4, (x + 3) % 4, (x + 2) % 4
    yp, ym, y2 = (y + 1) % 4, (y + 3) % 4, (y + 2) % 4
    cx = x % 2
    chunk = cx * 4 + y
    sibling = (z * 2 + (1 - core), col)

    def at(xx, yy):
        return (row, xx * 4 + yy)

    pair = at(x + 1 - 2 * cx, y)
    up, down = ((z + 1) % 4 * 2 + core, col), ((z + 3) % 4 * 2 + core, col)

    opposite = ((z + 2) % 4 * 2 + core, col)
    home = ((z + chunk // 2) % 4 * 2 + core, 2 * row + x // 2)
    is_home = jnp.logical_and(chunk // 2 == 0, home[1] == col)
    home_half = col % 2
    dz = (z - x + 4) % 4
    home_core = y // 2
    on_home_core = core == home_core

    own_loads = [pltpu.make_async_copy(src, dst, load.at[i]) for i, (src, dst) in enumerate((
        (right_ref, rtmp.at[0]), (left_ref, rtmp.at[1]), (inv_ref, l1.at[z])))]
    tile_loads = [pltpu.make_async_copy(src, dst, load.at[3 + i]) for i, (src, dst) in enumerate((
        (tiles_v, xv), (tiles_o, xo), (tiles_u, xu)))]
    for c in own_loads + tile_loads:
        c.start()

    bar = pltpu.get_barrier_semaphore()

    def greet(who, skip=None):
        if skip is None:
            pl.semaphore_signal(bar, inc=1, device_id=who, device_id_type=MESH)
        else:
            @pl.when(jnp.logical_not(skip))
            def _():
                pl.semaphore_signal(bar, inc=1, device_id=who, device_id_type=MESH)

    for who in (at(xp, y), at(xm, y), at(x, yp), at(x, ym), up, down, opposite, sibling):
        greet(who)
    for j in range(8):
        src = (z * 2 + chunk % 2, core * 8 + j)
        greet(src, jnp.logical_and(src[0] == row, src[1] == col))

    @pl.when(on_home_core)
    def _():
        for j in range(2):
            src = (2 * x + core, home_half * 8 + 2 * dz + j)
            greet(src, jnp.logical_and(src[0] == row, src[1] == col))

    l_self = jnp.logical_and(chunk % 2 == core, x // 2 == core)

    for c in own_loads:
        c.wait()
    rank = jnp.where(x // 2 == 0, rank_ref[0], rank_ref[1])
    keep = lax.broadcasted_iota(jnp.int32, (256, 256), 1) < rank
    rb[chunk] = jnp.where(keep, rtmp[0], 0.0)
    ug[x, y] = jnp.where(keep, rtmp[1], 0.0).reshape(2, 128, 256)
    pl.semaphore_wait(bar, 17 - jnp.where(l_self, 1, 0) - jnp.where(is_home, 1, 0))

    def remote(src, dst, ss, rs, who):
        return pltpu.make_async_remote_copy(
            src_ref=src, dst_ref=dst, send_sem=ss, recv_sem=rs, device_id=who, device_id_type=MESH)

    def send(buf, idx, ss, rs, i, who):
        remote(buf.at[idx], buf.at[idx], ss.at[i], rs.at[i], who).start()

    def arrive(buf, idx, rs, i):
        pltpu.make_async_copy(buf.at[idx], buf.at[idx], rs.at[i]).wait()

    def sent(buf, idx, ss, i):
        pltpu.make_async_copy(buf.at[idx], buf.at[idx], ss.at[i]).wait()

    own_c, pair_c = cx * 4, (1 - cx) * 4
    lo_half, hi_half = pl.ds(0, 128), pl.ds(128, 128)

    for i, who in enumerate((up, down, opposite)):
        remote(l1.at[z], l1.at[z], l1_s.at[i], l1_r.at[i], who).start()

    send(rb, chunk, r_s, r_r, 0, at(x, yp))
    send(rb, chunk, r_s, r_r, 1, at(x, ym))
    send(rb, chunk, r_s, r_r, 2, pair)

    def l_second():
        arrive(l1, (z + 3) % 4, l1_r, 0)
        arrive(l1, (z + 1) % 4, l1_r, 1)
        arrive(l1, (z + 2) % 4, l1_r, 2)
        for dzz in range(4):
            zz = (z + dzz) % 4
            c = 2 * zz + core
            for dx in range(2):
                who = (z * 2 + x // 2, (c // 4 + 2 * dx) * 4 + c % 4)
                me = jnp.logical_and(who[0] == row, who[1] == col)
                src = l1.at[zz]

                @pl.when(jnp.logical_not(me))
                def _():
                    remote(src, lb.at[l_piece], l_s.at[dzz * 2 + dx], l_r.at[j_own], who).start()

                @pl.when(me)
                def _():
                    pltpu.make_async_copy(src, lb.at[l_piece], l_r.at[j_own]).start()

    def l_finish():
        for i in range(3):
            pltpu.make_async_copy(l1.at[0], l1.at[0], l1_s.at[i]).wait()
        for dzz in range(4):
            c = 2 * ((z + dzz) % 4) + core
            for dx in range(2):
                me = jnp.logical_and(z * 2 + x // 2 == row, (c // 4 + 2 * dx) * 4 + c % 4 == col)

                @pl.when(jnp.logical_not(me))
                def _():
                    pltpu.make_async_copy(l1.at[0], l1.at[0], l_s.at[dzz * 2 + dx]).wait()

    l_piece = pl.ds(pl.multiple_of(col * 16, 16), 16)
    j_own = col % 8

    def gather(buf, ss, rs):
        done = []

        def snd(idx, i, who):
            send(buf, idx, ss, rs, i, who)
            done.append((idx, i))

        def arr(idx, i):
            arrive(buf, idx, rs, i)

        q0, q1 = pl.ds(0, 64), pl.ds(64, 64)
        XP, XM, YP, YM = at(xp, y), at(xm, y), at(x, yp), at(x, ym)

        def s0():
            snd((x, y), 0, YP)
            snd((x, y), 1, YM)
            snd((x, y), 2, XP)
            snd((x, y), 3, XM)

        def s1():
            arr((x, ym), 0)
            snd((x, ym, 0, q0), 4, YP)
            snd((x, ym, 0), 5, XP)
            snd((x, ym, 0), 6, XM)
            snd((x, ym, 1, q0), 28, YP)

        def s2():
            arr((xm, y), 2)
            snd((xm, y, 1, q0), 20, XP)
            snd((xm, y, 1), 21, YP)
            snd((xm, y, 1), 22, YM)
            snd((xm, y, 0, q0), 12, XP)

        def s3():
            arr((x, yp), 1)
            snd((x, yp, 0, q1), 7, YM)
            snd((x, yp, 0), 8, XP)
            snd((x, yp, 0), 9, XM)
            snd((x, yp, 1, q1), 29, YM)

        def s4():
            arr((xp, y), 3)
            snd((xp, y, 1, q1), 23, XM)
            snd((xp, y, 1), 24, YP)
            snd((xp, y, 1), 25, YM)
            snd((xp, y, 0, q1), 13, XM)

        def s5():
            arr((x, y2, 0, q0), 4)
            arr((x, y2, 0, q1), 7)
            snd((x, y2, 0), 10, XP)
            snd((x, y2, 0), 11, XM)

        def s6():
            arr((x2, y, 1, q0), 20)
            arr((x2, y, 1, q1), 23)
            snd((x2, y, 1), 26, YP)
            snd((x2, y, 1), 27, YM)

        def s7():
            arr((xm, ym, 0), 5)
            snd((xm, ym, 0, q0), 14, XP)
            arr((xp, ym, 0), 6)
            snd((xp, ym, 0, q1), 15, XM)
            arr((xm, ym, 1), 21)
            snd((xm, ym, 1, q0), 30, YP)
            arr((xm, yp, 1), 22)
            snd((xm, yp, 1, q1), 31, YM)

        def s8():
            arr((xm, yp, 0), 8)
            snd((xm, yp, 0, q0), 16, XP)
            arr((xp, yp, 0), 9)
            snd((xp, yp, 0, q1), 17, XM)
            arr((xp, ym, 1), 24)
            snd((xp, ym, 1, q0), 32, YP)
            arr((xp, yp, 1), 25)
            snd((xp, yp, 1, q1), 33, YM)

        def s9():
            arr((xm, y2, 0), 10)
            snd((xm, y2, 0, q0), 18, XP)
            arr((xp, y2, 0), 11)
            snd((xp, y2, 0, q1), 19, XM)
            arr((x2, ym, 1), 26)
            snd((x2, ym, 1, q0), 34, YP)
            arr((x2, yp, 1), 27)
            snd((x2, yp, 1, q1), 35, YM)

        def s10():
            arr((x2, y, 0, q0), 12)
            arr((x2, y, 0, q1), 13)
            arr((x, y2, 1, q0), 28)
            arr((x, y2, 1, q1), 29)
            arr((x2, ym, 0, q0), 14)
            arr((x2, ym, 0, q1), 15)
            arr((xm, y2, 1, q0), 30)
            arr((xm, y2, 1, q1), 31)

        def s11():
            arr((x2, yp, 0, q0), 16)
            arr((x2, yp, 0, q1), 17)
            arr((xp, y2, 1, q0), 32)
            arr((xp, y2, 1, q1), 33)
            arr((x2, y2, 0, q0), 18)
            arr((x2, y2, 0, q1), 19)
            arr((x2, y2, 1, q0), 34)
            arr((x2, y2, 1, q1), 35)

        def finish():
            for idx, i in done:
                sent(buf, idx, ss, i)

        return [s0, s1, s2, s3, s4, s5, s6, s7, s8, s9, s10, s11], finish

    halves = [pl.ds(0, 128), pl.ds(128, 128)]

    def to_home(buf, qbuf, os, orr):
        for hh in range(2):
            @pl.when(jnp.logical_not(is_home))
            def _():
                remote(buf.at[x, y, hh], qbuf.at[chunk, halves[hh]], os.at[hh], orr.at[2 * chunk + hh], home).start()

            @pl.when(is_home)
            def _():
                pltpu.make_async_copy(buf.at[x, y, hh], qbuf.at[chunk, halves[hh]], orr.at[2 * chunk + hh]).start()

    def to_home_finish(buf, os):
        for hh in range(2):
            @pl.when(jnp.logical_not(is_home))
            def _():
                pltpu.make_async_copy(buf.at[x, y, hh], buf.at[x, y, hh], os.at[hh]).wait()

    def ring(qbuf, orr, zs, zr, cs, cr):
        idx_of = lambda k: (k // 2, halves[k % 2])
        carries = lambda k: core == (home_core + k) % 2
        onward = lambda k: up if (k // 2) % 2 == 0 else down
        off = lambda k: (dz + 4 - k // 4) % 4
        hop_of = lambda k: off(k) if (k // 2) % 2 == 0 else (4 - off(k)) % 4
        at_source = lambda k: jnp.logical_and(off(k) == 0, on_home_core)

        def src(k):
            idx = idx_of(k)

            @pl.when(at_source(k))
            def _():
                arrive(qbuf, idx, orr, k)
                if k % 2 == 0:
                    send(qbuf, idx, zs, zr, k, onward(k))
                send(qbuf, idx, cs, cr, k, sibling)

            if k % 2 == 1:
                @pl.when(jnp.logical_and(off(k) == 0, jnp.logical_not(on_home_core)))
                def _():
                    arrive(qbuf, idx, cr, k)
                    send(qbuf, idx, zs, zr, k, onward(k))

        def hop(number, k):
            idx = idx_of(k)

            @pl.when(jnp.logical_and(hop_of(k) == number, carries(k)))
            def _():
                arrive(qbuf, idx, zr, k)
                if number < 3:
                    send(qbuf, idx, zs, zr, k, onward(k))
                send(qbuf, idx, cs, cr, k, sibling)

        def end(k):
            waits = jnp.logical_and(jnp.logical_not(carries(k)), jnp.logical_not(at_source(k)))

            @pl.when(waits)
            def _():
                arrive(qbuf, idx_of(k), cr, k)

        def finish():
            for k in range(16):
                idx = idx_of(k)

                @pl.when(jnp.logical_and(carries(k), hop_of(k) != 3))
                def _():
                    sent(qbuf, idx, zs, k)

                @pl.when(jnp.logical_or(at_source(k), jnp.logical_and(off(k) != 0, carries(k))))
                def _():
                    sent(qbuf, idx, cs, k)

        return src, hop, end, finish

    u_steps, u_finish = gather(ug, u_s, u_r)
    w_steps, w_finish = gather(wg, w_s, w_r)
    uz_src, uz_hop, uz_end, uz_finish = ring(uq, uo_r, uz_s, uz_r, uc_s, uc_r)
    wz_src, wz_hop, wz_end, wz_finish = ring(wq, wo_r, wz_s, wz_r, wc_s, wc_r)

    def pick(options, n):
        value = options[0]
        for i in range(1, len(options)):
            value = jnp.where(n == i, options[i], value)
        return value

    def right_probe(t):
        cc[t, :256] = jnp.zeros((256, 256), f32)

        @pl.loop(0, 4)
        def _(j):
            rows = pl.ds(pl.multiple_of(t * 2048 + j * 512, 512), 512)
            cc[t, :256] += dot6(xv[rows, :].T, xo[rows, :])

    def panel_probe(t):
        cc[t, 256:] = jnp.zeros((256, 256), f32)

        @pl.loop(0, 4)
        def _(j):
            rows = pl.ds(pl.multiple_of(t * 2048 + j * 512, 512), 512)
            cc[t, 256:] += dot6(uq[pl.ds(2 * j, 2)].reshape(512, 256).T, xo[rows, :])

    def cross(t):
        acc[...] = jnp.zeros_like(acc)

        @pl.loop(0, 4)
        def _(i):
            w = wg[2 * t + i // 2, pl.ds((i % 2) * 2, 2)].reshape(512, 256)
            acc[...] += dot6(w.T, wq[pl.ds(2 * i, 2)].reshape(512, 256))

        core_out[t] = acc[...] * (1.0 / 2048)

    def squares(places):
        @pl.loop(0, len(places))
        def _(n):
            px, py = pick([p[0] for p in places], n), pick([p[1] for p in places], n)
            rows = pl.ds(pl.multiple_of((px * 4 + py) * 256, 256), 256)
            t = px // 2
            x0, x1 = split2(jnp.concatenate([xu[rows, :], ug[px, py].reshape(256, 256)], axis=1))
            x0t = x0.T
            hh[t] += mul(x0t, x0)
            hl[t] += mul(x0t, x1)

    U = lambda *ks: [u_steps[k]() for k in ks]
    W = lambda *ks: [w_steps[k]() for k in ks]
    every = lambda fn, ks=range(16): [fn(k) for k in ks]

    to_home(ug, uq, uo_s, uo_r)
    l_second()
    tile_loads[0].wait()
    tile_loads[1].wait()
    right_probe(0)
    arrive(rb, own_c + ym, r_r, 0)
    send(rb, (own_c + ym, lo_half), r_s, r_r, 5, at(x, yp))
    arrive(rb, own_c + yp, r_r, 1)
    send(rb, (own_c + yp, hi_half), r_s, r_r, 6, at(x, ym))
    arrive(rb, pair_c + y, r_r, 2)
    send(rb, pair_c + y, r_s, r_r, 3, at(x, yp))
    send(rb, pair_c + y, r_s, r_r, 4, at(x, ym))
    arrive(rb, (own_c + y2, lo_half), r_r, 5)
    arrive(rb, (own_c + y2, hi_half), r_r, 6)
    send(rb, own_c + y2, r_s, r_r, 7, pair)
    for j in range(8):
        arrive(lb, pl.ds(pl.multiple_of(core * 128 + j * 16, 16), 16), l_r, j)
    my_half = pl.ds(pl.multiple_of(core * 128, 128), 128)
    other_half = pl.ds(pl.multiple_of(128 - core * 128, 128), 128)
    send(lb, my_half, lf_s, lf_r, 0, sibling)
    U(0)
    right_probe(1)
    tile_loads[2].wait()
    hh[...] = jnp.zeros_like(hh)
    hl[...] = jnp.zeros_like(hl)
    every(uz_src)
    arrive(rb, pair_c + ym, r_r, 3)
    arrive(rb, pair_c + yp, r_r, 4)
    arrive(rb, pair_c + y2, r_r, 7)
    arrive(lb, other_half, lf_r, 0)
    acc[...] = jnp.zeros_like(acc)

    @pl.loop(0, 8)
    def _(j):
        low = lb[:, pl.ds(pl.multiple_of(j * 256, 256), 256)]
        h0, h1, h2 = split3(rb[j])
        acc[...] += (mul(low, h2) + mul(low, h1)) + mul(low, h0)

    wg[x, y] = acc[...].reshape(2, 128, 256)
    W(0)
    to_home(wg, wq, wo_s, wo_r)
    hop = lambda fn, number: [fn(number, k) for k in range(16)]
    hop(uz_hop, 1)
    W(1, 2, 3, 4)
    every(wz_src)
    hop(uz_hop, 2)
    W(5, 6, 7, 8)
    hop(wz_hop, 1)
    hop(uz_hop, 3)
    W(9)
    U(1, 2, 3, 4)
    hop(wz_hop, 2)
    every(uz_end)
    panel_probe(0)
    U(5, 6)
    hop(wz_hop, 3)
    squares([(x, y), (x, ym), (xm, y), (x, yp), (xp, y)])
    U(7, 8)
    panel_probe(1)
    U(9)
    W(10, 11)
    every(wz_end)
    cross(0)
    cross(1)
    U(10)
    squares([(xm, ym), (xp, ym), (xm, yp), (xp, yp), (x2, y), (x, y2), (x2, ym), (xm, y2)])
    U(11)
    outs = [pltpu.make_async_copy(src, dst, loc.at[i]) for i, (src, dst) in enumerate((
        (ug, ug_out), (uq, uq_out), (cc, cc_out), (hh, hh_out)))]
    for c in outs[:3]:
        c.start()
    squares([(x2, yp), (xp, y2), (x2, y2)])
    for t in range(2):
        hh[t] += hl[t] + hl[t].T
    outs[3].start()
    sent(rb, chunk, r_s, 0)
    sent(rb, chunk, r_s, 1)
    sent(rb, chunk, r_s, 2)
    sent(rb, pair_c + y, r_s, 3)
    sent(rb, pair_c + y, r_s, 4)
    sent(rb, (own_c + ym, lo_half), r_s, 5)
    sent(rb, (own_c + yp, hi_half), r_s, 6)
    sent(rb, own_c + y2, r_s, 7)
    sent(lb, my_half, lf_s, 0)
    l_finish()

    u_finish()
    w_finish()
    uz_finish()
    to_home_finish(ug, uo_s)
    wz_finish()
    to_home_finish(wg, wo_s)
    for c in outs:
        c.wait()


def run_exchange(panel_rank, factor_inverse, panel_right, panel_left, left, right, probes):
    dma = pltpu.SemaphoreType.DMA
    vm = pl.BlockSpec(memory_space=pltpu.VMEM)
    hbm = pl.BlockSpec(memory_space=pl.ANY)
    shape = lambda *dims: jax.ShapeDtypeStruct(dims, f32)
    return pl.pallas_call(
        exchange,
        out_shape=(shape(4, 4, 2, 128, 256), shape(8, 256, 256), shape(2, 256, 256), shape(2, 512, 512), shape(2, 512, 256)),
        in_specs=[pl.BlockSpec(memory_space=pltpu.SMEM)] + [hbm] * 6,
        out_specs=(hbm, hbm, vm, hbm, hbm),
        scratch_shapes=[
            pltpu.VMEM((8, 256, 256), f32), pltpu.VMEM((4, 16, 2048), bf16), pltpu.VMEM((256, 2048), bf16),
            pltpu.VMEM((4, 4, 2, 128, 256), f32), pltpu.VMEM((8, 256, 256), f32),
            pltpu.VMEM((4, 4, 2, 128, 256), f32), pltpu.VMEM((8, 256, 256), f32),
            pltpu.VMEM((256, 256), f32), pltpu.VMEM((2, 256, 256), f32),
            pltpu.VMEM((4096, 256), f32), pltpu.VMEM((4096, 256), f32), pltpu.VMEM((4096, 256), f32),
            pltpu.VMEM((2, 512, 512), f32), pltpu.VMEM((2, 512, 512), f32), pltpu.VMEM((2, 512, 256), f32),
            dma((3,)), dma((3,)), dma((8,)), dma((8,)), dma((1,)), dma((1,)), dma((8,)), dma((8,)),
            dma((36,)), dma((36,)), dma((36,)), dma((36,)),
            dma((2,)), dma((16,)), dma((16,)), dma((16,)), dma((16,)), dma((16,)),
            dma((2,)), dma((16,)), dma((16,)), dma((16,)), dma((16,)), dma((16,)),
            dma((4,)), dma((6,)),
        ],
        compiler_params=pltpu.CompilerParams(collective_id=0, has_side_effects=True, vmem_limit_bytes=56 << 20),
        name="exchange",
    )(panel_rank, factor_inverse, panel_right, panel_left, left, right, probes)


def split2(a):
    hi = a.astype(bf16)
    return hi, (a - hi.astype(f32)).astype(bf16)


def mul(a, b):
    return jnp.dot(a, b, preferred_element_type=f32)


def dot3(a, b):
    a0, a1 = split2(a)
    b0, b1 = split2(b)
    return (mul(a0, b1) + mul(a1, b0)) + mul(a0, b0)


def dot6(a, b):
    a0, a1, a2 = split3(a)
    b0, b1, b2 = split3(b)
    small = mul(a1, b1) + mul(a0, b2) + mul(a2, b0)
    return (small + (mul(a0, b1) + mul(a1, b0))) + mul(a0, b0)


NB = 64


def factor_blocks(blocks):
    sub = lax.broadcasted_iota(jnp.int32, (8, 128), 0)
    lane = lax.broadcasted_iota(jnp.int32, (8, 128), 1)
    n = NB // 8
    all_rows = []
    for block in blocks:
        rows = []
        for g in range(n):
            unit = jnp.where(lane == sub + (NB + 8 * g), 1.0, 0.0)
            rows.append(jnp.concatenate([block[8 * g:8 * g + 8, :], unit[:, NB:]], axis=1))
        all_rows.append(rows)
    scales = [[None] * n for _ in blocks]
    for k in range(n):
        wide = [[[jnp.broadcast_to(rows[g][:, 8 * k + i:8 * k + i + 1], (8, 128)) for i in range(8)] if g >= k else None for g in range(n)] for rows in all_rows]
        pivots = [jnp.zeros((8, 128), f32) for _ in blocks]
        for i in range(8):
            for b, rows in enumerate(all_rows):
                w = wide[b]
                pivot = jnp.broadcast_to(w[k][i][i:i + 1, :], (8, 128))
                inverse = 1.0 / pivot
                pivots[b] = jnp.where(sub == i, pivot, pivots[b])
                row = jnp.broadcast_to(rows[k][i:i + 1, :], (8, 128))
                heads = [jnp.broadcast_to(w[k][j][i:i + 1, :], (8, 128)) for j in range(i + 1, 8)]
                for g in range(k, n):
                    factor = w[g][i] * inverse
                    if g == k:
                        factor = jnp.where(sub > i, factor, 0.0)
                    for j in range(i + 1, 8):
                        w[g][j] = w[g][j] - factor * heads[j - i - 1]
                    rows[g] = rows[g] - factor * row
        for b in range(len(blocks)):
            scales[b][k] = lax.rsqrt(pivots[b])
    return [jnp.concatenate([rows[g] * scales[b][g] for g in range(n)], axis=0)[:, NB:] for b, rows in enumerate(all_rows)]


def solve_rows(g_refs, c_refs):
    count = len(g_refs)
    for k in range(256 // NB):
        lo, hi = k * NB, (k + 1) * NB
        inverses = factor_blocks([g[lo:hi, lo:hi] for g in g_refs])
        for b in range(count):
            g, c = g_refs[b], c_refs[b]
            if hi < 256:
                gu = dot6(inverses[b], g[lo:hi, hi:])
            cu = dot6(inverses[b], c[lo:hi, :])
            c[lo:hi, :] = cu
            if hi < 256:
                gt = gu.T
                g[hi:, hi:] -= dot6(gt, gu)
                c[hi:, :] -= dot6(gt, cu)


CHUNK = 512


def tiles_kernel(rank_ref, left, right, ug, uq, core_in, hh_in, cc_in, out_left, out_right,
                 xu, xv, xg, xq, yl, yr, core, hh, cc, gg, ct, ds0, ds1, es0, es1, in_sem, out_sem):
    order = 2048
    copies = [pltpu.make_async_copy(src, dst, in_sem.at[i]) for i, (src, dst) in enumerate((
        (core_in, core), (cc_in, cc), (hh_in, hh), (left, xu), (ug, xg), (right, xv), (uq, xq)))]
    for c in copies:
        c.start()
    columns = lax.broadcasted_iota(jnp.int32, (256, 256), 1)
    rows_at = lax.broadcasted_iota(jnp.int32, (256, 256), 0)
    for c in copies[:3]:
        c.wait()
    for t in range(2):
        keep = columns < rank_ref[t]
        scale = 1.0 / order
        c1 = jnp.where(jnp.logical_and(keep, rows_at < rank_ref[t]), cc[t, :256], 0.0) * scale
        pp = jnp.where(keep, cc[t, 256:], 0.0) * -scale
        c2 = dot6(core[t], pp)
        c = jnp.concatenate([c1, c2], axis=0)
        ct[t] = c.T
        hc = dot6(hh[t], c)
        unit = jnp.where(jnp.logical_and(columns == rows_at, jnp.logical_not(keep)), 1.0, 0.0)
        gg[t] = dot6(ct[t], hc) + unit
    solve_rows([gg.at[0], gg.at[1]], [ct.at[0], ct.at[1]])
    for c in copies[3:]:
        c.wait()
    stores = []
    for t in range(2):
        rank = rank_ref[t]
        d = (ct[t] * math.sqrt(order)).T
        d0, d1 = split2(d)
        ds0[t], ds1[t] = d0, d1
        h0, h1 = split2(hh[t])
        hd = (mul(h0, d1) + mul(h1, d0)) + mul(h0, d0)
        e1 = jnp.where(rows_at < rank, hd[:256], 0.0) * (1.0 / order)
        e2 = dot3(core[t].T, hd[256:]) * (-1.0 / order)
        es0[t], es1[t] = split2(jnp.concatenate([e1, e2], axis=0))

        @pl.loop(0, order // CHUNK, unroll=2)
        def _(j):
            at = pl.ds(pl.multiple_of(t * order + j * CHUNK, CHUNK), CHUNK)
            x0, x1 = split2(jnp.concatenate([xu[at, :], xg[at, :]], axis=1))
            yl[at, :] = (mul(x0, ds1[t]) + mul(x1, ds0[t])) + mul(x0, ds0[t])

        rows = pl.ds(t * order, order)
        stores.append(pltpu.make_async_copy(yl.at[rows], out_left.at[rows], out_sem.at[2 * t]))
        stores[-1].start()

        @pl.loop(0, order // CHUNK, unroll=2)
        def _(j):
            at = pl.ds(pl.multiple_of(t * order + j * CHUNK, CHUNK), CHUNK)
            atq = pl.ds(pl.multiple_of(j * CHUNK, CHUNK), CHUNK)
            x0, x1 = split2(jnp.concatenate([xv[at, :], xq[atq, :]], axis=1))
            yr[at, :] = (mul(x0, es1[t]) + mul(x1, es0[t])) + mul(x0, es0[t])

        stores.append(pltpu.make_async_copy(yr.at[rows], out_right.at[rows], out_sem.at[2 * t + 1]))
        stores[-1].start()
    for store in stores:
        store.wait()


def run_tiles(trail_rank, left, right, ug, uq, core, hh, cc):
    hbm = pl.BlockSpec(memory_space=pl.ANY)
    big = pltpu.VMEM((4096, 256), f32)
    return pl.pallas_call(
        tiles_kernel,
        out_shape=(jax.ShapeDtypeStruct((4096, 256), f32),) * 2,
        in_specs=[pl.BlockSpec(memory_space=pltpu.SMEM)] + [hbm] * 7,
        out_specs=(hbm, hbm),
        scratch_shapes=[big, big, big, pltpu.VMEM((2048, 256), f32), big, big, pltpu.VMEM((2, 256, 256), f32),
                        pltpu.VMEM((2, 512, 512), f32), pltpu.VMEM((2, 512, 256), f32),
                        pltpu.VMEM((2, 256, 256), f32), pltpu.VMEM((2, 256, 512), f32)]
        + [pltpu.VMEM((2, 512, 256), bf16)] * 4
        + [pltpu.SemaphoreType.DMA((7,)), pltpu.SemaphoreType.DMA((4,))],
        compiler_params=pltpu.CompilerParams(vmem_limit_bytes=56 << 20),
        name="tiles",
    )(trail_rank, left, right, ug, uq, core, hh, cc)


def shards(factor_inverse, panel_left, panel_right, panel_rank, left, right, probes, trail_rank):
    ug, uq, core, hh, cc = run_exchange(panel_rank, factor_inverse, panel_right, panel_left, left, right, probes)
    ug, uq = ug.reshape(4096, 256), uq.reshape(2048, 256)
    return run_tiles(trail_rank.reshape(-1), left, right, ug, uq, core, hh, cc)


def solution(mesh):
    return jax.shard_map(
        shards,
        mesh=mesh,
        in_specs=(
            P(("row", "col"), None),
            P(("row", "col"), None),
            P(("row", "col"), None),
            P("row"),
            P("row", "col"),
            P("row", "col"),
            P("row", "col"),
            P("row", "col"),
        ),
        out_specs=(P("row", "col"), P("row", "col")),
        check_vma=False,
    )
```

```python
import functools
import math

import jax
import jax.numpy as jnp
from jax import lax
from jax.experimental import pallas as pl
from jax.experimental.pallas import tpu as pltpu
from jax.sharding import PartitionSpec as P

MESH = pl.DeviceIdType.MESH
f32, bf16 = jnp.float32, jnp.bfloat16


def split3(a):
    hi = a.astype(bf16)
    rest = a - hi.astype(f32)
    mid = rest.astype(bf16)
    return hi, mid, (rest - mid.astype(f32)).astype(bf16)


def exchange(rank_ref, inv_ref, right_ref, left_ref, tiles_u, tiles_v, tiles_o, ug_out, uq_out, core_out, hh_out, cc_out,
             rb, l1, lb, wg, wq, ug, uq, acc, rtmp, xu, xv, xo, hh, hl, cc,
             l1_s, l1_r, l_s, l_r, lf_s, lf_r, r_s, r_r, w_s, w_r, u_s, u_r,
             wo_s, wo_r, wz_s, wz_r, wc_s, wc_r, uo_s, uo_r, uz_s, uz_r, uc_s, uc_r, loc, load):
    row, col = lax.axis_index("row"), lax.axis_index("col")
    z, core = row // 2, row % 2
    x, y = col // 4, col % 4
    xp, xm, x2 = (x + 1) % 4, (x + 3) % 4, (x + 2) % 4
    yp, ym, y2 = (y + 1) % 4, (y + 3) % 4, (y + 2) % 4
    cx = x % 2
    chunk = cx * 4 + y
    sibling = (z * 2 + (1 - core), col)

    def at(xx, yy):
        return (row, xx * 4 + yy)

    pair = at(x + 1 - 2 * cx, y)
    up, down = ((z + 1) % 4 * 2 + core, col), ((z + 3) % 4 * 2 + core, col)

    opposite = ((z + 2) % 4 * 2 + core, col)
    home = ((z + chunk // 2) % 4 * 2 + core, 2 * row + x // 2)
    is_home = jnp.logical_and(chunk // 2 == 0, home[1] == col)
    home_half = col % 2
    dz = (z - x + 4) % 4
    home_core = y // 2
    on_home_core = core == home_core

    own_loads = [pltpu.make_async_copy(src, dst, load.at[i]) for i, (src, dst) in enumerate((
        (right_ref, rtmp.at[0]), (left_ref, rtmp.at[1]), (inv_ref, l1.at[z])))]
    tile_loads = [pltpu.make_async_copy(src, dst, load.at[3 + i]) for i, (src, dst) in enumerate((
        (tiles_v, xv), (tiles_o, xo), (tiles_u, xu)))]
    for c in own_loads:
        c.start()

    bar = pltpu.get_barrier_semaphore()

    def greet(who, skip=None):
        if skip is None:
            pl.semaphore_signal(bar, inc=1, device_id=who, device_id_type=MESH)
        else:
            @pl.when(jnp.logical_not(skip))
            def _():
                pl.semaphore_signal(bar, inc=1, device_id=who, device_id_type=MESH)

    for who in (at(xp, y), at(xm, y), at(x, yp), at(x, ym), up, down, opposite, sibling):
        greet(who)
    for j in range(8):
        src = (z * 2 + chunk % 2, core * 8 + j)
        greet(src, jnp.logical_and(src[0] == row, src[1] == col))

    @pl.when(on_home_core)
    def _():
        for j in range(2):
            src = (2 * x + core, home_half * 8 + 2 * dz + j)
            greet(src, jnp.logical_and(src[0] == row, src[1] == col))

    l_self = jnp.logical_and(chunk % 2 == core, x // 2 == core)

    for c in own_loads:
        c.wait()
    for c in tile_loads:
        c.start()
    rank = jnp.where(x // 2 == 0, rank_ref[0], rank_ref[1])
    keep = lax.broadcasted_iota(jnp.int32, (256, 256), 1) < rank
    rb[chunk] = jnp.where(keep, rtmp[0], 0.0)
    ug[x, y] = jnp.where(keep, rtmp[1], 0.0).reshape(2, 128, 256)
    pl.semaphore_wait(bar, 17 - jnp.where(l_self, 1, 0) - jnp.where(is_home, 1, 0))

    def remote(src, dst, ss, rs, who):
        return pltpu.make_async_remote_copy(
            src_ref=src, dst_ref=dst, send_sem=ss, recv_sem=rs, device_id=who, device_id_type=MESH)

    def send(buf, idx, ss, rs, i, who):
        remote(buf.at[idx], buf.at[idx], ss.at[i], rs.at[i], who).start()

    def arrive(buf, idx, rs, i):
        pltpu.make_async_copy(buf.at[idx], buf.at[idx], rs.at[i]).wait()

    def sent(buf, idx, ss, i):
        pltpu.make_async_copy(buf.at[idx], buf.at[idx], ss.at[i]).wait()

    own_c, pair_c = cx * 4, (1 - cx) * 4
    lo_half, hi_half = pl.ds(0, 128), pl.ds(128, 128)

    for i, who in enumerate((up, down, opposite)):
        remote(l1.at[z], l1.at[z], l1_s.at[i], l1_r.at[i], who).start()

    send(rb, chunk, r_s, r_r, 0, at(x, yp))
    send(rb, chunk, r_s, r_r, 1, at(x, ym))
    send(rb, chunk, r_s, r_r, 2, pair)

    def l_second():
        arrive(l1, (z + 3) % 4, l1_r, 0)
        arrive(l1, (z + 1) % 4, l1_r, 1)
        arrive(l1, (z + 2) % 4, l1_r, 2)
        for dzz in range(4):
            zz = (z + dzz) % 4
            c = 2 * zz + core
            for dx in range(2):
                who = (z * 2 + x // 2, (c // 4 + 2 * dx) * 4 + c % 4)
                me = jnp.logical_and(who[0] == row, who[1] == col)
                src = l1.at[zz]

                @pl.when(jnp.logical_not(me))
                def _():
                    remote(src, lb.at[l_piece], l_s.at[dzz * 2 + dx], l_r.at[j_own], who).start()

                @pl.when(me)
                def _():
                    pltpu.make_async_copy(src, lb.at[l_piece], l_r.at[j_own]).start()

    def l_finish():
        for i in range(3):
            pltpu.make_async_copy(l1.at[0], l1.at[0], l1_s.at[i]).wait()
        for dzz in range(4):
            c = 2 * ((z + dzz) % 4) + core
            for dx in range(2):
                me = jnp.logical_and(z * 2 + x // 2 == row, (c // 4 + 2 * dx) * 4 + c % 4 == col)

                @pl.when(jnp.logical_not(me))
                def _():
                    pltpu.make_async_copy(l1.at[0], l1.at[0], l_s.at[dzz * 2 + dx]).wait()

    l_piece = pl.ds(pl.multiple_of(col * 16, 16), 16)
    j_own = col % 8

    def gather(buf, ss, rs):
        done = []

        def snd(idx, i, who):
            send(buf, idx, ss, rs, i, who)
            done.append((idx, i))

        def arr(idx, i):
            arrive(buf, idx, rs, i)

        q0, q1 = pl.ds(0, 64), pl.ds(64, 64)
        XP, XM, YP, YM = at(xp, y), at(xm, y), at(x, yp), at(x, ym)

        def s0():
            snd((x, y), 0, YP)
            snd((x, y), 1, YM)
            snd((x, y), 2, XP)
            snd((x, y), 3, XM)

        def s1():
            arr((x, ym), 0)
            snd((x, ym, 0, q0), 4, YP)
            snd((x, ym, 0), 5, XP)
            snd((x, ym, 0), 6, XM)
            snd((x, ym, 1, q0), 28, YP)

        def s2():
            arr((xm, y), 2)
            snd((xm, y, 1, q0), 20, XP)
            snd((xm, y, 1), 21, YP)
            snd((xm, y, 1), 22, YM)
            snd((xm, y, 0, q0), 12, XP)

        def s3():
            arr((x, yp), 1)
            snd((x, yp, 0, q1), 7, YM)
            snd((x, yp, 0), 8, XP)
            snd((x, yp, 0), 9, XM)
            snd((x, yp, 1, q1), 29, YM)

        def s4():
            arr((xp, y), 3)
            snd((xp, y, 1, q1), 23, XM)
            snd((xp, y, 1), 24, YP)
            snd((xp, y, 1), 25, YM)
            snd((xp, y, 0, q1), 13, XM)

        def s5():
            arr((x, y2, 0, q0), 4)
            arr((x, y2, 0, q1), 7)
            snd((x, y2, 0), 10, XP)
            snd((x, y2, 0), 11, XM)

        def s6():
            arr((x2, y, 1, q0), 20)
            arr((x2, y, 1, q1), 23)
            snd((x2, y, 1), 26, YP)
            snd((x2, y, 1), 27, YM)

        def s7():
            arr((xm, ym, 0), 5)
            snd((xm, ym, 0, q0), 14, XP)
            arr((xp, ym, 0), 6)
            snd((xp, ym, 0, q1), 15, XM)
            arr((xm, ym, 1), 21)
            snd((xm, ym, 1, q0), 30, YP)
            arr((xm, yp, 1), 22)
            snd((xm, yp, 1, q1), 31, YM)

        def s8():
            arr((xm, yp, 0), 8)
            snd((xm, yp, 0, q0), 16, XP)
            arr((xp, yp, 0), 9)
            snd((xp, yp, 0, q1), 17, XM)
            arr((xp, ym, 1), 24)
            snd((xp, ym, 1, q0), 32, YP)
            arr((xp, yp, 1), 25)
            snd((xp, yp, 1, q1), 33, YM)

        def s9():
            arr((xm, y2, 0), 10)
            snd((xm, y2, 0, q0), 18, XP)
            arr((xp, y2, 0), 11)
            snd((xp, y2, 0, q1), 19, XM)
            arr((x2, ym, 1), 26)
            snd((x2, ym, 1, q0), 34, YP)
            arr((x2, yp, 1), 27)
            snd((x2, yp, 1, q1), 35, YM)

        def s10():
            arr((x2, y, 0, q0), 12)
            arr((x2, y, 0, q1), 13)
            arr((x, y2, 1, q0), 28)
            arr((x, y2, 1, q1), 29)
            arr((x2, ym, 0, q0), 14)
            arr((x2, ym, 0, q1), 15)
            arr((xm, y2, 1, q0), 30)
            arr((xm, y2, 1, q1), 31)

        def s11():
            arr((x2, yp, 0, q0), 16)
            arr((x2, yp, 0, q1), 17)
            arr((xp, y2, 1, q0), 32)
            arr((xp, y2, 1, q1), 33)
            arr((x2, y2, 0, q0), 18)
            arr((x2, y2, 0, q1), 19)
            arr((x2, y2, 1, q0), 34)
            arr((x2, y2, 1, q1), 35)

        def finish():
            for idx, i in done:
                sent(buf, idx, ss, i)

        return [s0, s1, s2, s3, s4, s5, s6, s7, s8, s9, s10, s11], finish

    halves = [pl.ds(0, 128), pl.ds(128, 128)]

    def to_home(buf, qbuf, os, orr):
        for hh in range(2):
            @pl.when(jnp.logical_not(is_home))
            def _():
                remote(buf.at[x, y, hh], qbuf.at[chunk, halves[hh]], os.at[hh], orr.at[2 * chunk + hh], home).start()

            @pl.when(is_home)
            def _():
                pltpu.make_async_copy(buf.at[x, y, hh], qbuf.at[chunk, halves[hh]], orr.at[2 * chunk + hh]).start()

    def to_home_finish(buf, os):
        for hh in range(2):
            @pl.when(jnp.logical_not(is_home))
            def _():
                pltpu.make_async_copy(buf.at[x, y, hh], buf.at[x, y, hh], os.at[hh]).wait()

    def ring(qbuf, orr, zs, zr, cs, cr):
        idx_of = lambda k: (k // 2, halves[k % 2])
        carries = lambda k: core == (home_core + k) % 2
        onward = lambda k: up if (k // 2) % 2 == 0 else down
        off = lambda k: (dz + 4 - k // 4) % 4
        hop_of = lambda k: off(k) if (k // 2) % 2 == 0 else (4 - off(k)) % 4
        at_source = lambda k: jnp.logical_and(off(k) == 0, on_home_core)

        def src(k):
            idx = idx_of(k)

            @pl.when(at_source(k))
            def _():
                arrive(qbuf, idx, orr, k)
                if k % 2 == 0:
                    send(qbuf, idx, zs, zr, k, onward(k))
                send(qbuf, idx, cs, cr, k, sibling)

            if k % 2 == 1:
                @pl.when(jnp.logical_and(off(k) == 0, jnp.logical_not(on_home_core)))
                def _():
                    arrive(qbuf, idx, cr, k)
                    send(qbuf, idx, zs, zr, k, onward(k))

        def hop(number, k):
            idx = idx_of(k)

            @pl.when(jnp.logical_and(hop_of(k) == number, carries(k)))
            def _():
                arrive(qbuf, idx, zr, k)
                if number < 3:
                    send(qbuf, idx, zs, zr, k, onward(k))
                send(qbuf, idx, cs, cr, k, sibling)

        def end(k):
            waits = jnp.logical_and(jnp.logical_not(carries(k)), jnp.logical_not(at_source(k)))

            @pl.when(waits)
            def _():
                arrive(qbuf, idx_of(k), cr, k)

        def finish():
            for k in range(16):
                idx = idx_of(k)

                @pl.when(jnp.logical_and(carries(k), hop_of(k) != 3))
                def _():
                    sent(qbuf, idx, zs, k)

                @pl.when(jnp.logical_or(at_source(k), jnp.logical_and(off(k) != 0, carries(k))))
                def _():
                    sent(qbuf, idx, cs, k)

        return src, hop, end, finish

    u_steps, u_finish = gather(ug, u_s, u_r)
    w_steps, w_finish = gather(wg, w_s, w_r)
    uz_src, uz_hop, uz_end, uz_finish = ring(uq, uo_r, uz_s, uz_r, uc_s, uc_r)
    wz_src, wz_hop, wz_end, wz_finish = ring(wq, wo_r, wz_s, wz_r, wc_s, wc_r)

    def pick(options, n):
        value = options[0]
        for i in range(1, len(options)):
            value = jnp.where(n == i, options[i], value)
        return value

    def right_probe(t):
        cc[t, :256] = jnp.zeros((256, 256), f32)

        @pl.loop(0, 4)
        def _(j):
            rows = pl.ds(pl.multiple_of(t * 2048 + j * 512, 512), 512)
            cc[t, :256] += dot6(xv[rows, :].T, xo[rows, :])

    def panel_probe(t):
        cc[t, 256:] = jnp.zeros((256, 256), f32)

        @pl.loop(0, 4)
        def _(j):
            rows = pl.ds(pl.multiple_of(t * 2048 + j * 512, 512), 512)
            cc[t, 256:] += dot6(uq[pl.ds(2 * j, 2)].reshape(512, 256).T, xo[rows, :])

    def cross(t):
        acc[...] = jnp.zeros_like(acc)

        @pl.loop(0, 4)
        def _(i):
            w = wg[2 * t + i // 2, pl.ds((i % 2) * 2, 2)].reshape(512, 256)
            acc[...] += dot6(w.T, wq[pl.ds(2 * i, 2)].reshape(512, 256))

        core_out[t] = acc[...] * (1.0 / 2048)

    def squares(places):
        @pl.loop(0, len(places))
        def _(n):
            px, py = pick([p[0] for p in places], n), pick([p[1] for p in places], n)
            rows = pl.ds(pl.multiple_of((px * 4 + py) * 256, 256), 256)
            t = px // 2
            x0, x1 = split2(jnp.concatenate([xu[rows, :], ug[px, py].reshape(256, 256)], axis=1))
            x0t = x0.T
            hh[t] += mul(x0t, x0)
            hl[t] += mul(x0t, x1)

    U = lambda *ks: [u_steps[k]() for k in ks]
    W = lambda *ks: [w_steps[k]() for k in ks]
    every = lambda fn, ks=range(16): [fn(k) for k in ks]

    to_home(ug, uq, uo_s, uo_r)
    l_second()
    tile_loads[0].wait()
    tile_loads[1].wait()
    right_probe(0)
    arrive(rb, own_c + ym, r_r, 0)
    send(rb, (own_c + ym, lo_half), r_s, r_r, 5, at(x, yp))
    arrive(rb, own_c + yp, r_r, 1)
    send(rb, (own_c + yp, hi_half), r_s, r_r, 6, at(x, ym))
    arrive(rb, pair_c + y, r_r, 2)
    send(rb, pair_c + y, r_s, r_r, 3, at(x, yp))
    send(rb, pair_c + y, r_s, r_r, 4, at(x, ym))
    arrive(rb, (own_c + y2, lo_half), r_r, 5)
    arrive(rb, (own_c + y2, hi_half), r_r, 6)
    send(rb, own_c + y2, r_s, r_r, 7, pair)
    for j in range(8):
        arrive(lb, pl.ds(pl.multiple_of(core * 128 + j * 16, 16), 16), l_r, j)
    my_half = pl.ds(pl.multiple_of(core * 128, 128), 128)
    other_half = pl.ds(pl.multiple_of(128 - core * 128, 128), 128)
    send(lb, my_half, lf_s, lf_r, 0, sibling)
    U(0)
    right_probe(1)
    tile_loads[2].wait()
    hh[...] = jnp.zeros_like(hh)
    hl[...] = jnp.zeros_like(hl)
    every(uz_src)
    arrive(rb, pair_c + ym, r_r, 3)
    arrive(rb, pair_c + yp, r_r, 4)
    arrive(rb, pair_c + y2, r_r, 7)
    arrive(lb, other_half, lf_r, 0)
    acc[...] = jnp.zeros_like(acc)

    @pl.loop(0, 8)
    def _(j):
        low = lb[:, pl.ds(pl.multiple_of(j * 256, 256), 256)]
        h0, h1, h2 = split3(rb[j])
        acc[...] += (mul(low, h2) + mul(low, h1)) + mul(low, h0)

    wg[x, y] = acc[...].reshape(2, 128, 256)
    W(0)
    to_home(wg, wq, wo_s, wo_r)
    hop = lambda fn, number: [fn(number, k) for k in range(16)]
    hop(uz_hop, 1)
    W(1, 2, 3, 4)
    every(wz_src)
    hop(uz_hop, 2)
    W(5, 6, 7, 8)
    hop(wz_hop, 1)
    hop(uz_hop, 3)
    W(9)
    U(1, 2, 3, 4)
    hop(wz_hop, 2)
    every(uz_end)
    panel_probe(0)
    U(5, 6)
    hop(wz_hop, 3)
    squares([(x, y), (x, ym), (xm, y), (x, yp), (xp, y)])
    U(7, 8)
    panel_probe(1)
    U(9)
    W(10, 11)
    every(wz_end)
    cross(0)
    cross(1)
    U(10)
    squares([(xm, ym), (xp, ym), (xm, yp), (xp, yp), (x2, y), (x, y2), (x2, ym), (xm, y2)])
    U(11)
    outs = [pltpu.make_async_copy(src, dst, loc.at[i]) for i, (src, dst) in enumerate((
        (ug, ug_out), (uq, uq_out), (cc, cc_out), (hh, hh_out)))]
    for c in outs[:3]:
        c.start()
    squares([(x2, yp), (xp, y2), (x2, y2)])
    for t in range(2):
        hh[t] += hl[t] + hl[t].T
    outs[3].start()
    sent(rb, chunk, r_s, 0)
    sent(rb, chunk, r_s, 1)
    sent(rb, chunk, r_s, 2)
    sent(rb, pair_c + y, r_s, 3)
    sent(rb, pair_c + y, r_s, 4)
    sent(rb, (own_c + ym, lo_half), r_s, 5)
    sent(rb, (own_c + yp, hi_half), r_s, 6)
    sent(rb, own_c + y2, r_s, 7)
    sent(lb, my_half, lf_s, 0)
    l_finish()

    u_finish()
    w_finish()
    uz_finish()
    to_home_finish(ug, uo_s)
    wz_finish()
    to_home_finish(wg, wo_s)
    for c in outs:
        c.wait()


def run_exchange(panel_rank, factor_inverse, panel_right, panel_left, left, right, probes):
    dma = pltpu.SemaphoreType.DMA
    vm = pl.BlockSpec(memory_space=pltpu.VMEM)
    hbm = pl.BlockSpec(memory_space=pl.ANY)
    shape = lambda *dims: jax.ShapeDtypeStruct(dims, f32)
    return pl.pallas_call(
        exchange,
        out_shape=(shape(4, 4, 2, 128, 256), shape(8, 256, 256), shape(2, 256, 256), shape(2, 512, 512), shape(2, 512, 256)),
        in_specs=[pl.BlockSpec(memory_space=pltpu.SMEM)] + [hbm] * 6,
        out_specs=(hbm, hbm, vm, hbm, hbm),
        scratch_shapes=[
            pltpu.VMEM((8, 256, 256), f32), pltpu.VMEM((4, 16, 2048), bf16), pltpu.VMEM((256, 2048), bf16),
            pltpu.VMEM((4, 4, 2, 128, 256), f32), pltpu.VMEM((8, 256, 256), f32),
            pltpu.VMEM((4, 4, 2, 128, 256), f32), pltpu.VMEM((8, 256, 256), f32),
            pltpu.VMEM((256, 256), f32), pltpu.VMEM((2, 256, 256), f32),
            pltpu.VMEM((4096, 256), f32), pltpu.VMEM((4096, 256), f32), pltpu.VMEM((4096, 256), f32),
            pltpu.VMEM((2, 512, 512), f32), pltpu.VMEM((2, 512, 512), f32), pltpu.VMEM((2, 512, 256), f32),
            dma((3,)), dma((3,)), dma((8,)), dma((8,)), dma((1,)), dma((1,)), dma((8,)), dma((8,)),
            dma((36,)), dma((36,)), dma((36,)), dma((36,)),
            dma((2,)), dma((16,)), dma((16,)), dma((16,)), dma((16,)), dma((16,)),
            dma((2,)), dma((16,)), dma((16,)), dma((16,)), dma((16,)), dma((16,)),
            dma((4,)), dma((6,)),
        ],
        compiler_params=pltpu.CompilerParams(collective_id=0, has_side_effects=True, vmem_limit_bytes=56 << 20),
        name="exchange",
    )(panel_rank, factor_inverse, panel_right, panel_left, left, right, probes)


def split2(a):
    hi = a.astype(bf16)
    return hi, (a - hi.astype(f32)).astype(bf16)


def mul(a, b):
    return jnp.dot(a, b, preferred_element_type=f32)


def dot3(a, b):
    a0, a1 = split2(a)
    b0, b1 = split2(b)
    return (mul(a0, b1) + mul(a1, b0)) + mul(a0, b0)


def dot6(a, b):
    a0, a1, a2 = split3(a)
    b0, b1, b2 = split3(b)
    small = mul(a1, b1) + mul(a0, b2) + mul(a2, b0)
    return (small + (mul(a0, b1) + mul(a1, b0))) + mul(a0, b0)


NB = 64


def factor_blocks(blocks):
    sub = lax.broadcasted_iota(jnp.int32, (8, 128), 0)
    lane = lax.broadcasted_iota(jnp.int32, (8, 128), 1)
    n = NB // 8
    all_rows = []
    for block in blocks:
        rows = []
        for g in range(n):
            unit = jnp.where(lane == sub + (NB + 8 * g), 1.0, 0.0)
            rows.append(jnp.concatenate([block[8 * g:8 * g + 8, :], unit[:, NB:]], axis=1))
        all_rows.append(rows)
    scales = [[None] * n for _ in blocks]
    for k in range(n):
        wide = [[[jnp.broadcast_to(rows[g][:, 8 * k + i:8 * k + i + 1], (8, 128)) for i in range(8)] if g >= k else None for g in range(n)] for rows in all_rows]
        pivots = [jnp.zeros((8, 128), f32) for _ in blocks]
        for i in range(8):
            for b, rows in enumerate(all_rows):
                w = wide[b]
                pivot = jnp.broadcast_to(w[k][i][i:i + 1, :], (8, 128))
                inverse = 1.0 / pivot
                pivots[b] = jnp.where(sub == i, pivot, pivots[b])
                row = jnp.broadcast_to(rows[k][i:i + 1, :], (8, 128))
                heads = [jnp.broadcast_to(w[k][j][i:i + 1, :], (8, 128)) for j in range(i + 1, 8)]
                for g in range(k, n):
                    factor = w[g][i] * inverse
                    if g == k:
                        factor = jnp.where(sub > i, factor, 0.0)
                    for j in range(i + 1, 8):
                        w[g][j] = w[g][j] - factor * heads[j - i - 1]
                    rows[g] = rows[g] - factor * row
        for b in range(len(blocks)):
            scales[b][k] = lax.rsqrt(pivots[b])
    return [jnp.concatenate([rows[g] * scales[b][g] for g in range(n)], axis=0)[:, NB:] for b, rows in enumerate(all_rows)]


def solve_rows(g_refs, c_refs):
    count = len(g_refs)
    for k in range(256 // NB):
        lo, hi = k * NB, (k + 1) * NB
        inverses = factor_blocks([g[lo:hi, lo:hi] for g in g_refs])
        for b in range(count):
            g, c = g_refs[b], c_refs[b]
            if hi < 256:
                gu = dot6(inverses[b], g[lo:hi, hi:])
            cu = dot6(inverses[b], c[lo:hi, :])
            c[lo:hi, :] = cu
            if hi < 256:
                gt = gu.T
                g[hi:, hi:] -= dot6(gt, gu)
                c[hi:, :] -= dot6(gt, cu)


CHUNK = 512


def tiles_kernel(rank_ref, left, right, ug, uq, core_in, hh_in, cc_in, out_left, out_right,
                 xu, xv, xg, xq, yl, yr, core, hh, cc, gg, ct, ds0, ds1, es0, es1, in_sem, out_sem):
    order = 2048
    copies = [pltpu.make_async_copy(src, dst, in_sem.at[i]) for i, (src, dst) in enumerate((
        (core_in, core), (cc_in, cc), (hh_in, hh), (left, xu), (ug, xg), (right, xv), (uq, xq)))]
    for c in copies[:3]:
        c.start()
    columns = lax.broadcasted_iota(jnp.int32, (256, 256), 1)
    rows_at = lax.broadcasted_iota(jnp.int32, (256, 256), 0)
    for c in copies[:3]:
        c.wait()
    for c in copies[3:]:
        c.start()
    for t in range(2):
        keep = columns < rank_ref[t]
        scale = 1.0 / order
        c1 = jnp.where(jnp.logical_and(keep, rows_at < rank_ref[t]), cc[t, :256], 0.0) * scale
        pp = jnp.where(keep, cc[t, 256:], 0.0) * -scale
        c2 = dot6(core[t], pp)
        c = jnp.concatenate([c1, c2], axis=0)
        ct[t] = c.T
        hc = dot6(hh[t], c)
        unit = jnp.where(jnp.logical_and(columns == rows_at, jnp.logical_not(keep)), 1.0, 0.0)
        gg[t] = dot6(ct[t], hc) + unit
    solve_rows([gg.at[0], gg.at[1]], [ct.at[0], ct.at[1]])
    for c in copies[3:]:
        c.wait()
    stores = []
    for t in range(2):
        rank = rank_ref[t]
        d = (ct[t] * math.sqrt(order)).T
        d0, d1 = split2(d)
        ds0[t], ds1[t] = d0, d1
        h0, h1 = split2(hh[t])
        hd = (mul(h0, d1) + mul(h1, d0)) + mul(h0, d0)
        e1 = jnp.where(rows_at < rank, hd[:256], 0.0) * (1.0 / order)
        e2 = dot3(core[t].T, hd[256:]) * (-1.0 / order)
        es0[t], es1[t] = split2(jnp.concatenate([e1, e2], axis=0))

        @pl.loop(0, order // CHUNK, unroll=2)
        def _(j):
            at = pl.ds(pl.multiple_of(t * order + j * CHUNK, CHUNK), CHUNK)
            x0, x1 = split2(jnp.concatenate([xu[at, :], xg[at, :]], axis=1))
            yl[at, :] = (mul(x0, ds1[t]) + mul(x1, ds0[t])) + mul(x0, ds0[t])

        rows = pl.ds(t * order, order)
        stores.append(pltpu.make_async_copy(yl.at[rows], out_left.at[rows], out_sem.at[2 * t]))
        stores[-1].start()

        @pl.loop(0, order // CHUNK, unroll=2)
        def _(j):
            at = pl.ds(pl.multiple_of(t * order + j * CHUNK, CHUNK), CHUNK)
            atq = pl.ds(pl.multiple_of(j * CHUNK, CHUNK), CHUNK)
            x0, x1 = split2(jnp.concatenate([xv[at, :], xq[atq, :]], axis=1))
            yr[at, :] = (mul(x0, es1[t]) + mul(x1, es0[t])) + mul(x0, es0[t])

        stores.append(pltpu.make_async_copy(yr.at[rows], out_right.at[rows], out_sem.at[2 * t + 1]))
        stores[-1].start()
    for store in stores:
        store.wait()


def run_tiles(trail_rank, left, right, ug, uq, core, hh, cc):
    hbm = pl.BlockSpec(memory_space=pl.ANY)
    big = pltpu.VMEM((4096, 256), f32)
    return pl.pallas_call(
        tiles_kernel,
        out_shape=(jax.ShapeDtypeStruct((4096, 256), f32),) * 2,
        in_specs=[pl.BlockSpec(memory_space=pltpu.SMEM)] + [hbm] * 7,
        out_specs=(hbm, hbm),
        scratch_shapes=[big, big, big, pltpu.VMEM((2048, 256), f32), big, big, pltpu.VMEM((2, 256, 256), f32),
                        pltpu.VMEM((2, 512, 512), f32), pltpu.VMEM((2, 512, 256), f32),
                        pltpu.VMEM((2, 256, 256), f32), pltpu.VMEM((2, 256, 512), f32)]
        + [pltpu.VMEM((2, 512, 256), bf16)] * 4
        + [pltpu.SemaphoreType.DMA((7,)), pltpu.SemaphoreType.DMA((4,))],
        compiler_params=pltpu.CompilerParams(vmem_limit_bytes=56 << 20),
        name="tiles",
    )(trail_rank, left, right, ug, uq, core, hh, cc)


def shards(factor_inverse, panel_left, panel_right, panel_rank, left, right, probes, trail_rank):
    ug, uq, core, hh, cc = run_exchange(panel_rank, factor_inverse, panel_right, panel_left, left, right, probes)
    ug, uq = ug.reshape(4096, 256), uq.reshape(2048, 256)
    return run_tiles(trail_rank.reshape(-1), left, right, ug, uq, core, hh, cc)


def solution(mesh):
    return jax.shard_map(
        shards,
        mesh=mesh,
        in_specs=(
            P(("row", "col"), None),
            P(("row", "col"), None),
            P(("row", "col"), None),
            P("row"),
            P("row", "col"),
            P("row", "col"),
            P("row", "col"),
            P("row", "col"),
        ),
        out_specs=(P("row", "col"), P("row", "col")),
        check_vma=False,
    )
```
